32 devices in a mesh: groups: 2 (over y), rows: 4 (over z), samples: 4 (over x, core).
Axes of the slice: x: 2, y: 2, z: 4, core: 2. Of those that a mesh axis runs over, the one named last changes fastest.
Arguments:
- ancestor: float32 [4096, 512], P(('groups', 'rows'), 'samples'), parts along dimension 0, may hold values from -6 to 6
- panels: float32 [2, 2, 1024, 256], P(None, None, 'rows', 'samples'), may hold values from -0.1875 to 0.1875
- row_map: int32 [2, 1024], P(None, 'rows'), may hold values from 0 to 511
- offsets: int32 [2], replicated, may hold values from 0 to 1536
- noise: float32 [4096, 512], P('groups', 'samples'), parts along dimension 0, may hold values from -6 to 6
- inverse: float32 [2, 2, 256, 256], P(None, None, 'rows'), as said below
- inner_link: float32 [2, 256, 256], P(None, 'rows'), may hold values from -0.375 to 0.375
- cross_link: float32 [2, 2, 256, 256], P(None, None, 'rows'), may hold values from -0.25 to 0.25
Outputs:
- solved: float32 [2, 2, 256, 1024], P(None, None, 'rows', ('groups', 'samples')), parts along dimension 3
The draws below stay inside these ranges and needn't reach their ends.
There are 2 independent parts, one for each index of `groups`. The reference program is written for one: setup_inputs(seed, part) draws one part's arguments, and reference() takes and returns one part's arrays. A program takes and returns all parts, laid end to end along the dimension named above; an argument that names none is the same for every part. Nothing has to cross between parts.
Inputs may be any that keep to these rules, and one draw needn't show every extreme that they name: inverse[p, b] is upper triangular: entry (i, j) is zero for j < i, and its diagonal is positive.
All inputs are finite; a program needn't handle non-finite values.
Results may differ from the reference program's by a relative error of at most 0.0003.
Values sent between devices are 32-bit elements; how exact they have to be, the bound alone decides.
No kernel may reach another device: no remote copies, remote signals or barrier semaphores. Data moves between devices by JAX's collectives and lax.ppermute only.
A program may use at most 64 MiB of HBM per device.

```python
import math
import jax
import jax.numpy as jnp
from jax import lax

BLOCK = 256
ROW_DEV = 256
ANC_DEV = 512
NOISE = 2048
PANEL = 512
FRONT = 1024
ANC = 2048
SAMPLES = 512


def draw_inverse(key, part):
    diag_key, upper_key = jax.random.split(jax.random.fold_in(key, 7))
    diagonal = jax.random.uniform(diag_key, (2, 2, BLOCK), jnp.float32, 0.5, 1.5)
    upper = jax.random.normal(upper_key, (2, 2, BLOCK, BLOCK), jnp.float32) / math.sqrt(BLOCK)
    row_ids = jnp.arange(BLOCK)[:, None]
    col_ids = jnp.arange(BLOCK)[None, :]
    above = col_ids > row_ids
    on_diag = (col_ids == row_ids).astype(jnp.float32)
    return jnp.where(above, upper, 0.0) + diagonal[..., None] * on_diag


def place_ends(array, rng, low, top_value):
    extent = array.shape
    spot = [jax.random.randint(jax.random.fold_in(rng, axis), (), 0, extent[axis]) for axis in range(len(extent))]
    array = array.at[tuple(spot)].set(low)
    longest = extent.index(max(extent))
    spot[longest] = (spot[longest] + 1) % extent[longest]
    return array.at[tuple(spot)].set(top_value)


def shard_levels(stream_key, extent, pieces, smallest, high):
    level = 1.0
    for position, shards_of in pieces:
        steps = jax.random.uniform(jax.random.fold_in(jax.random.fold_in(stream_key, 6), position), (shards_of,), jnp.float32, smallest / len(pieces), high / len(pieces))
        level = level * jnp.repeat(jnp.exp(steps), extent[position] // shards_of).reshape((-1,) + (1,) * (len(extent) - 1 - position))
    return level


def gaussian(rng, dims, spread, limit, pieces=(), held_as=jnp.bfloat16):
    drawn = jax.random.normal(rng, dims, jnp.float32) * spread
    if len(pieces) > 0:
        drawn = shard_levels(rng, dims, pieces, -0.22, 0.18) * drawn
    return jnp.clip(drawn, min=-limit, max=limit).astype(held_as)


def setup_inputs(seed: int = 0, part: int = 0) -> dict:
    arg_keys = jax.random.split(jax.random.key(seed), 9)
    part_keys = jax.random.split(jax.random.fold_in(arg_keys[8], part), 9)
    return {
        "ancestor": gaussian(part_keys[0], (ANC, SAMPLES), 1.0, 6.0, ((0, 4), (1, 4)), jnp.float32),
        "panels": gaussian(arg_keys[1], (2, 2, FRONT, BLOCK), FRONT ** -0.5, 0.1875, ((2, 4), (3, 4)), jnp.float32),
        "row_map": place_ends(jax.random.randint(arg_keys[2], (2, FRONT), 0, ANC_DEV), jax.random.fold_in(arg_keys[2], 1), 0, ANC_DEV - 1).astype(jnp.int32),
        "offsets": jax.random.randint(arg_keys[3], (2,), 0, NOISE - PANEL + 1).astype(jnp.int32),
        "noise": gaussian(part_keys[4], (NOISE, SAMPLES), 1.0, 6.0, ((1, 4),), jnp.float32),
        "inverse": draw_inverse(jax.random.fold_in(arg_keys[8], 71), part),
        "inner_link": gaussian(arg_keys[6], (2, BLOCK, BLOCK), BLOCK ** -0.5, 0.375, ((1, 4),), jnp.float32),
        "cross_link": gaussian(arg_keys[7], (2, 2, BLOCK, BLOCK), (2 * BLOCK) ** -0.5, 0.25, ((2, 4),), jnp.float32),
    }


def product(left, right):
    return jnp.dot(left, right, precision=lax.Precision.HIGHEST, preferred_element_type=jnp.float32)


def reference(ancestor, panels, row_map, offsets, noise, inverse, inner_link, cross_link):
    owners = (jnp.arange(FRONT, dtype=jnp.int32) // ROW_DEV) * ANC_DEV
    solved = [[None, None], [None, None]]
    for which_panel in (1, 0):
        indices = (row_map[which_panel] + owners).astype(jnp.int32)
        front_rows = jnp.take(ancestor, indices, axis=0)
        window = lax.dynamic_slice_in_dim(noise, offsets[which_panel], 2 * BLOCK, 0)
        for which_block in (1, 0):
            partial_value = product(panels[which_panel, which_block].T, front_rows)
            if which_block == 0:
                partial_value = partial_value + product(inner_link[which_panel].T, solved[which_panel][1])
            if which_panel == 0:
                for earlier in (0, 1):
                    partial_value = partial_value + product(cross_link[which_block, earlier].T, solved[1][earlier])
            target = window[which_block * BLOCK:(which_block + 1) * BLOCK]
            solved[which_panel][which_block] = product(inverse[which_panel, which_block], target - partial_value)
    return jnp.stack([jnp.stack(solved[0]), jnp.stack(solved[1])])
```

```python
import functools

import jax
import jax.numpy as jnp
from jax import lax
from jax.experimental import pallas as pl
from jax.experimental.pallas import tpu as pltpu
from jax.sharding import PartitionSpec as P

F32 = jnp.float32
HIGHEST = lax.Precision.HIGHEST
VMEM = pl.BlockSpec(memory_space=pltpu.VMEM)
SMEM = pl.BlockSpec(memory_space=pltpu.SMEM)


def product(left, right):
    return jnp.dot(left, right, precision=HIGHEST, preferred_element_type=F32)


def product_t(left, right):
    return lax.dot_general(
        left, right, (((1,), (1,)), ((), ())), precision=HIGHEST, preferred_element_type=F32
    )


def apply_inverse(target, partial_value, inverse_rows):
    rows_here = inverse_rows.shape[0]
    share = lax.psum_scatter(partial_value, "rows", scatter_dimension=0, tiled=True)
    first_own = lax.axis_index("rows") * rows_here
    residue = lax.dynamic_slice_in_dim(target, first_own, rows_here, 0) - share
    return product(inverse_rows, lax.all_gather(residue, "rows", axis=0, tiled=True))


def general(ancestor, panels, row_map, offsets, noise, inverse, inner_link, cross_link):
    block_rows = inverse.shape[3]
    solved = [[None, None], [None, None]]
    for p in (1, 0):
        front_rows = jnp.take(ancestor, row_map[p], axis=0)
        window = lax.dynamic_slice_in_dim(noise, offsets[p], 2 * block_rows, 0)
        for b in (1, 0):
            whole = lax.all_gather(panels[p, b], "samples", axis=1, tiled=True)
            partial_value = product(whole.T, front_rows)
            if b == 0:
                partial_value = partial_value + product(inner_link[p].T, solved[p][1])
            if p == 0:
                for earlier in (0, 1):
                    partial_value = partial_value + product(
                        cross_link[b, earlier].T, solved[1][earlier]
                    )
            target = window[b * block_rows : (b + 1) * block_rows]
            solved[p][b] = apply_inverse(target, partial_value, inverse[p, b])
    return jnp.stack([jnp.stack(solved[0]), jnp.stack(solved[1])])


def exchange(array, axis, mask, size):
    return lax.ppermute(array, axis, [(i, i ^ mask) for i in range(size)])


def pack_kernel(pos_ref, panels_ref, inv_ref, inner_ref, cross_ref, packed_ref, share_ref):
    for p in range(2):
        packed_ref[p] = jnp.concatenate([panels_ref[p, 0], panels_ref[p, 1]], axis=-1)
    share_ref[0:4] = inv_ref[...]
    share_ref[4:6] = inner_ref[...]
    share_ref[6:10] = cross_ref[...]


def pack(pos, panels, inverse, inner, cross, parts):
    k_rows, cols = panels.shape[2:]
    rows_here, block = inverse.shape[1:]
    piece = rows_here // parts

    def rows_of(count):
        return pl.BlockSpec((count, piece, block), lambda i, pos: (0, pos[3], 0))

    return pl.pallas_call(
        pack_kernel,
        out_shape=(
            jax.ShapeDtypeStruct((2, k_rows, 2 * cols), F32),
            jax.ShapeDtypeStruct((10, piece, block), F32),
        ),
        grid_spec=pltpu.PrefetchScalarGridSpec(
            num_scalar_prefetch=1,
            grid=(1,),
            in_specs=[
                pl.BlockSpec(panels.shape, lambda i, pos: (0, 0, 0, 0)),
                rows_of(4),
                rows_of(2),
                rows_of(4),
            ],
            out_specs=[
                pl.BlockSpec((2, k_rows, 2 * cols), lambda i, pos: (0, 0, 0)),
                pl.BlockSpec((10, piece, block), lambda i, pos: (0, 0, 0)),
            ],
        ),
        name="pack",
    )(pos, panels, inverse, inner, cross)


def terms(pos_ref, front_t, packed, out_refs, hold):
    row = pos_ref[0]
    ranks, quarter = hold.shape[0], hold.shape[1]
    width = packed[0].shape[2]
    for p in range(2):
        both = jnp.concatenate([ref[p] for ref in packed], axis=-1)
        value = product(front_t[p], both)
        hold[...] = value.reshape(ranks, quarter, value.shape[1])
        for k, out in enumerate(out_refs):
            piece = hold[row ^ k]
            for group in range(len(packed)):
                out[group, p] = piece[:, group * width : (group + 1) * width]


def first_terms_kernel(pos_ref, map_ref, ancestor_ref, own_ref, other_ref, front_ref, *rest):
    out_refs, (front, hold) = rest[:-2], rest[-2:]
    k_rows = front.shape[1]
    step = 8
    for p in range(2):

        def body(i, carry):
            base = pl.multiple_of(i * step, step)
            rows = [ancestor_ref[pl.ds(map_ref[p, base + j], 1), :] for j in range(step)]
            front[p, pl.ds(base, step), :] = jnp.concatenate(rows, axis=0)
            return carry

        lax.fori_loop(0, k_rows // step, body, 0, unroll=4)
    for p in range(2):
        front_ref[p] = front[p].T
    terms(pos_ref, front_ref, (own_ref, other_ref), out_refs, hold)


def first_terms(pos, row_map, ancestor, own, other, ranks):
    k_rows, width = own.shape[1:]
    cols_here = ancestor.shape[1]
    quarter = cols_here // ranks
    out = jax.ShapeDtypeStruct((2, 2, quarter, width), F32)
    return pl.pallas_call(
        first_terms_kernel,
        out_shape=(jax.ShapeDtypeStruct((2, cols_here, k_rows), F32),) + (out,) * ranks,
        in_specs=[SMEM, SMEM, VMEM, VMEM, VMEM],
        out_specs=(VMEM,) * (ranks + 1),
        scratch_shapes=[
            pltpu.VMEM((2, k_rows, cols_here), F32),
            pltpu.VMEM((ranks, quarter, 2 * width), F32),
        ],
        name="first_terms",
    )(pos, row_map, ancestor, own, other)


def second_terms_kernel(pos_ref, front_ref, left_ref, right_ref, *rest):
    out_refs, hold = rest[:-1], rest[-1]
    terms(pos_ref, front_ref, (left_ref, right_ref), out_refs, hold)


def second_terms(pos, front_t, left, right, ranks):
    width = left.shape[2]
    quarter = front_t.shape[1] // ranks
    out = jax.ShapeDtypeStruct((2, 2, quarter, width), F32)
    return pl.pallas_call(
        second_terms_kernel,
        out_shape=(out,) * ranks,
        in_specs=[SMEM, VMEM, VMEM, VMEM],
        out_specs=(VMEM,) * ranks,
        scratch_shapes=[pltpu.VMEM((ranks, quarter, 2 * width), F32)],
        name="second_terms",
    )(pos, front_t, left, right)


def target_kernel(pos_ref, one_ref, two_ref, out_ref, hold):
    ranks, quarter = hold.shape[0], hold.shape[1]
    for p, ref in enumerate((one_ref, two_ref)):
        turned = ref[...].T
        hold[...] = turned.reshape(ranks, quarter, turned.shape[1])
        out_ref[p] = hold[pos_ref[0]]


def targets(pos, windows, ranks):
    rows, cols_here = windows[0].shape
    quarter = cols_here // ranks
    return pl.pallas_call(
        target_kernel,
        out_shape=jax.ShapeDtypeStruct((2, quarter, rows), F32),
        in_specs=[SMEM, VMEM, VMEM],
        out_specs=VMEM,
        scratch_shapes=[pltpu.VMEM((ranks, quarter, rows), F32)],
        name="targets",
    )(pos, *windows)


def solve_kernel(ranks, samples, masks, *refs):
    refs = list(refs)
    pos_ref, target_ref = refs[:2]
    first = refs[2 : 2 + ranks]
    second = refs[2 + ranks : 2 + 2 * ranks]
    at = 2 + 2 * ranks
    inv_ref, inner_ref, cross_ref = refs[at : at + 3]
    at += 3
    shares = refs[at : at + len(masks)]
    at += len(masks)
    outs = refs[at : at + ranks]
    sums, mats, ordered = refs[at + ranks :]

    row, sample, group = pos_ref[0], pos_ref[1], pos_ref[2]
    rows_here, block = inv_ref.shape[1:]
    piece = shares[0].shape[2]
    own = pl.ds(pl.multiple_of(row * rows_here, rows_here), rows_here)
    mats[0:4, own, :] = inv_ref[...]
    mats[4:6, own, :] = inner_ref[...]
    mats[6:10, own, :] = cross_ref[...]
    for (group_mask, sample_mask), ref in zip(masks, shares):
        part = (group ^ group_mask) * samples + (sample ^ sample_mask)
        for k in range(1, ranks):
            start = (row ^ k) * rows_here + part * piece
            mats[:, pl.ds(pl.multiple_of(start, piece), piece), :] = ref[k - 1]

    half = samples // 2
    for stage, pieces in ((0, first), (1, second)):
        for position in range(half):
            total = pieces[0][position]
            for ref in pieces[1:]:
                total = total + ref[position]
            sums[sample ^ (stage * half + position)] = total
    cols = block // samples
    rest = [[None, None], [None, None]]
    for p in range(2):
        for b in range(2):
            value = jnp.concatenate(
                [sums[s, p, :, b * cols : (b + 1) * cols] for s in range(samples)], axis=-1
            )
            rest[p][b] = target_ref[p, :, b * block : (b + 1) * block] - value

    x11 = product_t(rest[1][1], mats[3])
    x10 = product_t(rest[1][0] - product(x11, mats[5]), mats[2])
    x01 = product_t(
        rest[0][1] - product(x11, mats[9]) - product(x10, mats[8]), mats[1]
    )
    x00 = product_t(
        rest[0][0] - product(x11, mats[7]) - product(x10, mats[6]) - product(x01, mats[4]),
        mats[0],
    )
    for j in range(ranks):
        ordered[j] = jnp.concatenate(
            [x[:, j * rows_here : (j + 1) * rows_here] for x in (x00, x01, x10, x11)], axis=-1
        )
    for k, out in enumerate(outs):
        out[...] = ordered[row ^ k]


def solve(pos, target, first, second, inverse, inner, cross, masks, shares, samples):
    ranks = len(first)
    quarter = target.shape[1]
    rows_here, block = inverse.shape[1:]
    out = jax.ShapeDtypeStruct((quarter, 4 * rows_here), F32)
    return pl.pallas_call(
        functools.partial(solve_kernel, ranks, samples, masks),
        out_shape=(out,) * ranks,
        in_specs=[SMEM] + [VMEM] * (1 + 2 * ranks + 3 + len(shares)),
        out_specs=(VMEM,) * ranks,
        scratch_shapes=[
            pltpu.VMEM((samples, 2, quarter, 2 * block // samples), F32),
            pltpu.VMEM((10, block, block), F32),
            pltpu.VMEM((ranks, quarter, 4 * rows_here), F32),
        ],
        name="solve",
    )(pos, target, *first, *second, inverse, inner, cross, *shares)


def place_kernel(ranks, *refs):
    pos_ref, pieces, out_ref, hold = refs[0], refs[1 : 1 + ranks], refs[1 + ranks], refs[2 + ranks]
    for k, ref in enumerate(pieces):
        hold[pos_ref[0] ^ k] = ref[...]
    quarter, width = hold.shape[1:]
    turned = hold[...].reshape(ranks * quarter, width).T
    rows_here = out_ref.shape[2]
    for p in range(2):
        for b in range(2):
            start = (2 * p + b) * rows_here
            out_ref[p, b] = turned[start : start + rows_here]


def place(pos, pieces):
    ranks = len(pieces)
    quarter, width = pieces[0].shape
    return pl.pallas_call(
        functools.partial(place_kernel, ranks),
        out_shape=jax.ShapeDtypeStruct((2, 2, width // 4, ranks * quarter), F32),
        in_specs=[SMEM] + [VMEM] * ranks,
        out_specs=VMEM,
        scratch_shapes=[pltpu.VMEM((ranks, quarter, width), F32)],
        name="place",
    )(pos, *pieces)


def paired(groups, ranks, samples):
    def local(ancestor, panels, row_map, offsets, noise, inverse, inner_link, cross_link):
        row, sample, group = (lax.axis_index(a) for a in ("rows", "samples", "groups"))
        pos = jnp.stack([row, sample, group, group * samples + sample]).astype(jnp.int32)
        block = inverse.shape[3]
        inverse = inverse.reshape((4,) + inverse.shape[2:])
        cross = cross_link.reshape((4,) + cross_link.shape[2:])

        own, share = pack(pos, panels, inverse, inner_link, cross, groups * samples)
        far = exchange(own, "samples", 2, samples)
        near = exchange(own, "samples", 1, samples)
        got = [exchange(share, "rows", k, ranks) for k in range(1, ranks)]
        windows = [lax.dynamic_slice_in_dim(noise, offsets[p], 2 * block, 0) for p in range(2)]

        front_t, *first = first_terms(pos, row_map, ancestor, own, near, ranks)
        first = [first[0]] + [exchange(first[k], "rows", k, ranks) for k in range(1, ranks)]
        far_near = exchange(far, "samples", 1, samples)
        second = second_terms(pos, front_t, far, far_near, ranks)
        second = [second[0]] + [exchange(second[k], "rows", k, ranks) for k in range(1, ranks)]
        target = targets(pos, windows, ranks)

        here = jnp.stack(got)
        over_x = exchange(here, "samples", 2, samples)
        over_y = exchange(here, "groups", 1, groups)
        over_xy = exchange(over_x, "groups", 1, groups)
        masks = [(0, 0), (0, 2), (1, 0), (1, 2)]
        shares = [here, over_x, over_y, over_xy]
        shares = shares + [exchange(a, "samples", 1, samples) for a in shares]
        masks = masks + [(g, s ^ 1) for g, s in masks]

        pieces = solve(
            pos, target, first, second, inverse, inner_link, cross, tuple(masks), shares, samples
        )
        pieces = [pieces[0]] + [exchange(pieces[k], "rows", k, ranks) for k in range(1, ranks)]
        return place(pos, pieces)

    return local


def solution(mesh):
    groups, ranks, samples = (mesh.shape[a] for a in ("groups", "rows", "samples"))
    placed = (
        P(("groups", "rows"), "samples"),
        P(None, None, "rows", "samples"),
        P(None, "rows"),
        P(),
        P("groups", "samples"),
        P(None, None, "rows", None),
        P(None, "rows", None),
        P(None, None, "rows", None),
    )

    def whole(*arrays):
        block, columns = arrays[5].shape[3], arrays[0].shape[1]
        fits = (
            groups == 2
            and samples == 4
            and ranks in (2, 4)
            and block % (ranks * groups * samples * 8) == 0
            and columns % (samples * ranks * 8) == 0
        )
        return jax.shard_map(
            paired(groups, ranks, samples) if fits else general,
            mesh=mesh,
            in_specs=placed,
            out_specs=P(None, None, "rows", ("groups", "samples")),
            check_vma=False,
        )(*arrays)

    return whole
```

```python
import functools

import jax
import jax.numpy as jnp
from jax import lax
from jax.experimental import pallas as pl
from jax.experimental.pallas import tpu as pltpu
from jax.sharding import PartitionSpec as P

F32 = jnp.float32
HIGHEST = lax.Precision.HIGHEST
B16 = jnp.bfloat16
VMEM = pl.BlockSpec(memory_space=pltpu.VMEM)
SMEM = pl.BlockSpec(memory_space=pltpu.SMEM)
ANY = pl.BlockSpec(memory_space=pl.ANY)


def product(left, right):
    return jnp.dot(left, right, precision=HIGHEST, preferred_element_type=F32)


def apply_inverse(target, partial_value, inverse_rows):
    rows_here = inverse_rows.shape[0]
    share = lax.psum_scatter(partial_value, "rows", scatter_dimension=0, tiled=True)
    first_own = lax.axis_index("rows") * rows_here
    residue = lax.dynamic_slice_in_dim(target, first_own, rows_here, 0) - share
    return product(inverse_rows, lax.all_gather(residue, "rows", axis=0, tiled=True))


def general(ancestor, panels, row_map, offsets, noise, inverse, inner_link, cross_link):
    block_rows = inverse.shape[3]
    solved = [[None, None], [None, None]]
    for p in (1, 0):
        front_rows = jnp.take(ancestor, row_map[p], axis=0)
        window = lax.dynamic_slice_in_dim(noise, offsets[p], 2 * block_rows, 0)
        for b in (1, 0):
            whole = lax.all_gather(panels[p, b], "samples", axis=1, tiled=True)
            partial_value = product(whole.T, front_rows)
            if b == 0:
                partial_value = partial_value + product(inner_link[p].T, solved[p][1])
            if p == 0:
                for earlier in (0, 1):
                    partial_value = partial_value + product(
                        cross_link[b, earlier].T, solved[1][earlier]
                    )
            target = window[b * block_rows : (b + 1) * block_rows]
            solved[p][b] = apply_inverse(target, partial_value, inverse[p, b])
    return jnp.stack([jnp.stack(solved[0]), jnp.stack(solved[1])])


def exchange(array, axis, mask, size):
    return lax.ppermute(array, axis, [(i, i ^ mask) for i in range(size)])


def near_core(array):
    return pltpu.with_memory_space_constraint(array, pltpu.VMEM)


def params():
    return pltpu.CompilerParams(vmem_limit_bytes=16 * 2**20)


def cost(flops, moved):
    return pl.CostEstimate(flops=flops, bytes_accessed=moved, transcendentals=0)


def halves(value):
    high = value.astype(B16)
    return high, (value - high.astype(F32)).astype(B16)


def dot_t(left, right):
    return lax.dot_general(left, right, (((1,), (1,)), ((), ())), preferred_element_type=F32)


def dot_n(left, right):
    return lax.dot_general(left, right, (((1,), (0,)), ((), ())), preferred_element_type=F32)


def stacked(dot, left, high, low):
    rows = left.shape[0]
    left_high, left_low = halves(left)
    value = dot(jnp.concatenate([left_high, left_low], axis=0), high)
    return value[:rows] + value[rows:] + dot(left_high, low)


def share_kernel(parts, samples, inv_ref, inner_ref, cross_ref, share_ref, sems):
    piece = share_ref.shape[1]
    part = lax.axis_index("groups") * samples + lax.axis_index("samples")
    rows = pl.ds(pl.multiple_of(part * piece, piece), piece)
    copies = []
    at = 0
    for i, ref in enumerate((inv_ref, inner_ref, cross_ref)):
        count = ref.shape[0]
        copies.append(
            pltpu.make_async_copy(
                ref.at[:, rows, :], share_ref.at[at : at + count], sems.at[i]
            )
        )
        at += count
    for copy in copies:
        copy.start()
    for copy in copies:
        copy.wait()


def own_share(inverse, inner, cross, groups, samples):
    parts = groups * samples
    rows_here, block = inverse.shape[1:]
    return pl.pallas_call(
        functools.partial(share_kernel, parts, samples),
        out_shape=pltpu.VMEM((10, rows_here // parts, block), F32),
        in_specs=[ANY] * 3,
        out_specs=VMEM,
        scratch_shapes=[pltpu.SemaphoreType.DMA((3,))],
        compiler_params=params(),
        name="own_share",
    )(inverse, inner, cross)


def front_kernel(map_ref, ancestor_ref, high_ref, low_ref, front):
    k_rows = front.shape[1]
    step = 8
    for p in range(2):

        def body(i, carry):
            base = pl.multiple_of(i * step, step)
            rows = [ancestor_ref[pl.ds(map_ref[p, base + j], 1), :] for j in range(step)]
            front[p, pl.ds(base, step), :] = jnp.concatenate(rows, axis=0)
            return carry

        lax.fori_loop(0, k_rows // step, body, 0, unroll=8)
        high_ref[p], low_ref[p] = halves(front[p].T)


def front_rows(row_map, ancestor):
    k_rows, cols_here = row_map.shape[1], ancestor.shape[1]
    out = pltpu.VMEM((2, cols_here, k_rows), B16)
    return pl.pallas_call(
        front_kernel,
        out_shape=(out, out),
        in_specs=[SMEM, VMEM],
        out_specs=(VMEM, VMEM),
        scratch_shapes=[pltpu.VMEM((2, k_rows, cols_here), F32)],
        cost_estimate=cost(2**22, 2**20),
        compiler_params=params(),
        name="front_rows",
    )(row_map, near_core(ancestor))


def terms_kernel(high_ref, low_ref, one_ref, two_ref, *rest):
    out_refs, hold = rest[:-1], rest[-1]
    row = lax.axis_index("rows")
    ranks, quarter = hold.shape[0], hold.shape[1]
    width = one_ref.shape[1]
    for p in range(2):
        high, low = halves(jnp.concatenate([one_ref[p], two_ref[p]], axis=0))
        value = dot_t(high_ref[p], high) + (dot_t(high_ref[p], low) + dot_t(low_ref[p], high))
        hold[...] = value.reshape(ranks, quarter, value.shape[1])
        for k, out in enumerate(out_refs):
            piece = hold[row ^ k]
            for group in range(2):
                out[group, p] = piece[:, group * width : (group + 1) * width]


def terms(front, one, two, ranks):
    width = one.shape[1]
    quarter = front[0].shape[1] // ranks
    out = pltpu.VMEM((2, 2, quarter, width), F32)
    return pl.pallas_call(
        terms_kernel,
        out_shape=(out,) * ranks,
        in_specs=[VMEM] * 4,
        out_specs=(VMEM,) * ranks,
        scratch_shapes=[pltpu.VMEM((ranks, quarter, 2 * width), F32)],
        cost_estimate=cost(2**26, 2**20),
        compiler_params=params(),
        name="terms",
    )(*front, near_core(one), near_core(two))


def target_kernel(off_ref, noise_ref, out_ref, window, hold, sems):
    ranks, quarter, rows = hold.shape
    span = window.shape[1]
    copies, shifts = [], []
    for p in range(2):
        offset = jnp.clip(off_ref[p], 0, noise_ref.shape[0] - rows)
        start = jnp.minimum((offset // 8) * 8, noise_ref.shape[0] - span)
        shifts.append(offset - start)
        copies.append(
            pltpu.make_async_copy(
                noise_ref.at[pl.ds(pl.multiple_of(start, 8), span), :], window.at[p], sems.at[p]
            )
        )
    for copy in copies:
        copy.start()
    for p in range(2):
        copies[p].wait()
        turned = window[p, pl.ds(shifts[p], rows), :].T
        hold[...] = turned.reshape(ranks, quarter, rows)
        out_ref[p] = hold[lax.axis_index("rows")]


def targets(offsets, noise, rows, ranks):
    cols_here = noise.shape[1]
    quarter = cols_here // ranks
    return pl.pallas_call(
        target_kernel,
        out_shape=pltpu.VMEM((2, quarter, rows), F32),
        in_specs=[SMEM, ANY],
        out_specs=VMEM,
        scratch_shapes=[
            pltpu.VMEM((2, rows + 8, cols_here), F32),
            pltpu.VMEM((ranks, quarter, rows), F32),
            pltpu.SemaphoreType.DMA((2,)),
        ],
        cost_estimate=cost(2**22, 2**20),
        compiler_params=params(),
        name="targets",
    )(offsets, noise)


def assemble_kernel(ranks, samples, masks, inv_ref, inner_ref, cross_ref, *rest):
    shares, (high_ref, low_ref, mats) = rest[: len(masks)], rest[len(masks) :]
    row, sample, group = (lax.axis_index(a) for a in ("rows", "samples", "groups"))
    rows_here = inv_ref.shape[1]
    piece = shares[0].shape[2]
    own = pl.ds(pl.multiple_of(row * rows_here, rows_here), rows_here)
    mats[0:4, own, :] = inv_ref[...]
    mats[4:6, own, :] = inner_ref[...]
    mats[6:10, own, :] = cross_ref[...]
    for (group_mask, sample_mask), ref in zip(masks, shares):
        part = (group ^ group_mask) * samples + (sample ^ sample_mask)
        for k in range(1, ranks):
            start = (row ^ k) * rows_here + part * piece
            mats[:, pl.ds(pl.multiple_of(start, piece), piece), :] = ref[k - 1]
    for m in range(10):
        high_ref[m], low_ref[m] = halves(mats[m])


def assemble(inverse, inner, cross, masks, shares, ranks, samples):
    block = inverse.shape[2]
    out = pltpu.VMEM((10, block, block), B16)
    return pl.pallas_call(
        functools.partial(assemble_kernel, ranks, samples, masks),
        out_shape=(out, out),
        in_specs=[VMEM] * (3 + len(shares)),
        out_specs=(VMEM, VMEM),
        scratch_shapes=[pltpu.VMEM((10, block, block), F32)],
        cost_estimate=cost(2**22, 2**22),
        compiler_params=params(),
        name="assemble",
    )(*(near_core(a) for a in (inverse, inner, cross, *shares)))


def solve_kernel(ranks, samples, target_ref, high_ref, low_ref, *refs):
    first, second = refs[:ranks], refs[ranks : 2 * ranks]
    outs, (sums, ordered) = refs[2 * ranks : 3 * ranks], refs[3 * ranks :]
    row, sample = lax.axis_index("rows"), lax.axis_index("samples")
    block = high_ref.shape[1]
    rows_here = block // ranks
    half = samples // 2
    for stage, pieces in ((0, first), (1, second)):
        for position in range(half):
            total = pieces[0][position]
            for ref in pieces[1:]:
                total = total + ref[position]
            sums[sample ^ (stage * half + position)] = total
    cols = block // samples
    rest = [[None, None], [None, None]]
    for p in range(2):
        for b in range(2):
            value = jnp.concatenate(
                [sums[s, p, :, b * cols : (b + 1) * cols] for s in range(samples)], axis=-1
            )
            rest[p][b] = target_ref[p, :, b * block : (b + 1) * block] - value

    def apply(value, m):
        return stacked(dot_t, value, high_ref[m], low_ref[m])

    def link(value, m):
        return stacked(dot_n, value, high_ref[m], low_ref[m])

    x11 = apply(rest[1][1], 3)
    x10 = apply(rest[1][0] - link(x11, 5), 2)
    x01 = apply(rest[0][1] - link(x11, 9) - link(x10, 8), 1)
    x00 = apply(rest[0][0] - link(x11, 7) - link(x10, 6) - link(x01, 4), 0)
    for j in range(ranks):
        ordered[j] = jnp.concatenate(
            [x[:, j * rows_here : (j + 1) * rows_here] for x in (x00, x01, x10, x11)], axis=-1
        )
    for k, out in enumerate(outs):
        out[...] = ordered[row ^ k]


def solve(target, mats, first, second, samples):
    ranks = len(first)
    quarter = target.shape[1]
    block = mats[0].shape[1]
    out = pltpu.VMEM((quarter, 4 * block // ranks), F32)
    return pl.pallas_call(
        functools.partial(solve_kernel, ranks, samples),
        out_shape=(out,) * ranks,
        in_specs=[VMEM] * (3 + 2 * ranks),
        out_specs=(VMEM,) * ranks,
        scratch_shapes=[
            pltpu.VMEM((samples, 2, quarter, 2 * block // samples), F32),
            pltpu.VMEM((ranks, quarter, 4 * block // ranks), F32),
        ],
        cost_estimate=cost(2**26, 2**21),
        compiler_params=params(),
        name="solve",
    )(*(near_core(a) for a in (target, *mats, *first, *second)))


def place_kernel(ranks, *refs):
    pieces, out_ref, hold = refs[:ranks], refs[ranks], refs[ranks + 1]
    for k, ref in enumerate(pieces):
        hold[lax.axis_index("rows") ^ k] = ref[...]
    quarter, width = hold.shape[1:]
    turned = hold[...].reshape(ranks * quarter, width).T
    rows_here = out_ref.shape[2]
    for p in range(2):
        for b in range(2):
            start = (2 * p + b) * rows_here
            out_ref[p, b] = turned[start : start + rows_here]


def place(pieces):
    ranks = len(pieces)
    quarter, width = pieces[0].shape
    return pl.pallas_call(
        functools.partial(place_kernel, ranks),
        out_shape=jax.ShapeDtypeStruct((2, 2, width // 4, ranks * quarter), F32),
        in_specs=[VMEM] * ranks,
        out_specs=VMEM,
        scratch_shapes=[pltpu.VMEM((ranks, quarter, width), F32)],
        compiler_params=params(),
        name="place",
    )(*(near_core(a) for a in pieces))


def paired(groups, ranks, samples):
    def over_rows(pieces):
        return [pieces[0]] + [exchange(pieces[k], "rows", k, ranks) for k in range(1, ranks)]

    def local(ancestor, panels, row_map, offsets, noise, inverse, inner_link, cross_link):
        block = inverse.shape[3]
        inverse = inverse.reshape((4,) + inverse.shape[2:])
        cross = cross_link.reshape((4,) + cross_link.shape[2:])
        own = jnp.swapaxes(panels, 2, 3)
        own = own.reshape((2, 2 * own.shape[2], own.shape[3]))

        share = own_share(inverse, inner_link, cross, groups, samples)
        far = exchange(own, "samples", 2, samples)
        near = exchange(own, "samples", 1, samples)
        got = [exchange(share, "rows", k, ranks) for k in range(1, ranks)]
        front = front_rows(row_map, ancestor)
        target = targets(offsets, noise, 2 * block, ranks)

        first = over_rows(terms(front, own, near, ranks))
        far_near = exchange(far, "samples", 1, samples)
        second = over_rows(terms(front, far, far_near, ranks))

        here = jnp.stack(got)
        over_x = exchange(here, "samples", 2, samples)
        over_y = exchange(here, "groups", 1, groups)
        over_xy = exchange(over_x, "groups", 1, groups)
        masks = [(0, 0), (0, 2), (1, 0), (1, 2)]
        shares = [here, over_x, over_y, over_xy]
        shares = shares + [exchange(a, "samples", 1, samples) for a in shares]
        masks = masks + [(g, s ^ 1) for g, s in masks]
        mats = assemble(inverse, inner_link, cross, tuple(masks), shares, ranks, samples)

        return place(over_rows(solve(target, mats, first, second, samples)))

    return local


def solution(mesh):
    groups, ranks, samples = (mesh.shape[a] for a in ("groups", "rows", "samples"))
    placed = (
        P(("groups", "rows"), "samples"),
        P(None, None, "rows", "samples"),
        P(None, "rows"),
        P(),
        P("groups", "samples"),
        P(None, None, "rows", None),
        P(None, "rows", None),
        P(None, None, "rows", None),
    )

    def whole(*arrays):
        block, columns = arrays[5].shape[3], arrays[0].shape[1]
        fits = (
            groups == 2
            and samples == 4
            and ranks in (2, 4)
            and block % (ranks * groups * samples * 8) == 0
            and columns % (samples * ranks * 8) == 0
        )
        return jax.shard_map(
            paired(groups, ranks, samples) if fits else general,
            mesh=mesh,
            in_specs=placed,
            out_specs=P(None, None, "rows", ("groups", "samples")),
            check_vma=False,
        )(*arrays)

    return whole
```

```python
import functools

import jax
import jax.numpy as jnp
from jax import lax
from jax.experimental import pallas as pl
from jax.experimental.pallas import tpu as pltpu
from jax.sharding import PartitionSpec as P

F32 = jnp.float32
HIGHEST = lax.Precision.HIGHEST
B16 = jnp.bfloat16
VMEM = pl.BlockSpec(memory_space=pltpu.VMEM)
SMEM = pl.BlockSpec(memory_space=pltpu.SMEM)
ANY = pl.BlockSpec(memory_space=pl.ANY)


def product(left, right):
    return jnp.dot(left, right, precision=HIGHEST, preferred_element_type=F32)


def apply_inverse(target, partial_value, inverse_rows):
    rows_here = inverse_rows.shape[0]
    share = lax.psum_scatter(partial_value, "rows", scatter_dimension=0, tiled=True)
    first_own = lax.axis_index("rows") * rows_here
    residue = lax.dynamic_slice_in_dim(target, first_own, rows_here, 0) - share
    return product(inverse_rows, lax.all_gather(residue, "rows", axis=0, tiled=True))


def general(ancestor, panels, row_map, offsets, noise, inverse, inner_link, cross_link):
    block_rows = inverse.shape[3]
    solved = [[None, None], [None, None]]
    for p in (1, 0):
        front_rows = jnp.take(ancestor, row_map[p], axis=0)
        window = lax.dynamic_slice_in_dim(noise, offsets[p], 2 * block_rows, 0)
        for b in (1, 0):
            whole = lax.all_gather(panels[p, b], "samples", axis=1, tiled=True)
            partial_value = product(whole.T, front_rows)
            if b == 0:
                partial_value = partial_value + product(inner_link[p].T, solved[p][1])
            if p == 0:
                for earlier in (0, 1):
                    partial_value = partial_value + product(
                        cross_link[b, earlier].T, solved[1][earlier]
                    )
            target = window[b * block_rows : (b + 1) * block_rows]
            solved[p][b] = apply_inverse(target, partial_value, inverse[p, b])
    return jnp.stack([jnp.stack(solved[0]), jnp.stack(solved[1])])


def exchange(array, axis, mask, size):
    return lax.ppermute(array, axis, [(i, i ^ mask) for i in range(size)])


def with_after(kernel, count, after):
    extra = len(after)

    def body(*refs):
        return kernel(*refs[:count], *refs[count + extra :])

    return body


def near_core(array):
    return pltpu.with_memory_space_constraint(array, pltpu.VMEM)


def far_memory(array):
    return pltpu.with_memory_space_constraint(array, pltpu.HBM)


def params():
    return pltpu.CompilerParams(vmem_limit_bytes=16 * 2**20)


def cost(flops, moved):
    return pl.CostEstimate(flops=flops, bytes_accessed=moved, transcendentals=0)


def halves(value):
    high = value.astype(B16)
    return high, (value - high.astype(F32)).astype(B16)


def dot_t(left, right):
    return lax.dot_general(left, right, (((1,), (1,)), ((), ())), preferred_element_type=F32)


def dot_n(left, right):
    return lax.dot_general(left, right, (((1,), (0,)), ((), ())), preferred_element_type=F32)


def stacked(dot, left, high, low):
    rows = left.shape[0]
    left_high, left_low = halves(left)
    value = dot(jnp.concatenate([left_high, left_low], axis=0), high)
    return value[:rows] + value[rows:] + dot(left_high, low)


def share_kernel(samples, *refs):
    sources, (share_ref, *fetched), sems = refs[:5], refs[5:8], refs[8]
    inv_ref, inner_ref, cross_ref, *whole = sources
    piece = share_ref.shape[1]
    part = lax.axis_index("groups") * samples + lax.axis_index("samples")
    rows = pl.ds(pl.multiple_of(part * piece, piece), piece)
    pairs, at = [], 0
    for ref in (inv_ref, inner_ref, cross_ref):
        pairs.append((ref.at[:, rows, :], share_ref.at[at : at + ref.shape[0]]))
        at += ref.shape[0]
    pairs += list(zip(whole, fetched))
    copies = [pltpu.make_async_copy(*pair, sems.at[i]) for i, pair in enumerate(pairs)]
    for copy in copies:
        copy.start()
    for copy in copies:
        copy.wait()


def own_share(inverse, inner, cross, whole, groups, samples):
    parts = groups * samples
    rows_here, block = inverse.shape[1:]
    return pl.pallas_call(
        functools.partial(share_kernel, samples),
        out_shape=(pltpu.VMEM((10, rows_here // parts, block), F32),)
        + tuple(pltpu.VMEM(a.shape, a.dtype) for a in whole),
        in_specs=[ANY] * (3 + len(whole)),
        out_specs=(VMEM,) * (1 + len(whole)),
        scratch_shapes=[pltpu.SemaphoreType.DMA((3 + len(whole),))],
        compiler_params=params(),
        cost_estimate=cost(1, 1),
        name="own_share",
    )(*(far_memory(a) for a in (inverse, inner, cross, *whole)))


def front_kernel(map_ref, ancestor_ref, high_ref, low_ref, front):
    k_rows = front.shape[1]
    step = 8
    for p in range(2):

        def body(i, carry):
            base = pl.multiple_of(i * step, step)
            rows = [ancestor_ref[pl.ds(map_ref[p, base + j], 1), :] for j in range(step)]
            front[p, pl.ds(base, step), :] = jnp.concatenate(rows, axis=0)
            return carry

        lax.fori_loop(0, k_rows // step, body, 0, unroll=8)
        high_ref[p], low_ref[p] = halves(front[p].T)


def front_rows(row_map, ancestor):
    k_rows, cols_here = row_map.shape[1], ancestor.shape[1]
    out = pltpu.VMEM((2, cols_here, k_rows), B16)
    return pl.pallas_call(
        front_kernel,
        out_shape=(out, out),
        in_specs=[SMEM, VMEM],
        out_specs=(VMEM, VMEM),
        scratch_shapes=[pltpu.VMEM((2, k_rows, cols_here), F32)],
        cost_estimate=cost(1, 1),
        compiler_params=params(),
        name="front_rows",
    )(far_memory(row_map), near_core(ancestor))


def gather_kernel(count, *refs):
    pieces, out_ref = refs[:count], refs[-1]
    at = 0
    for ref in pieces:
        out_ref[at : at + ref.shape[0]] = ref[...]
        at += ref.shape[0]


def gathered(pieces, after):
    total = sum(piece.shape[0] for piece in pieces)
    return pl.pallas_call(
        functools.partial(gather_kernel, len(pieces)),
        out_shape=pltpu.VMEM((total,) + pieces[0].shape[1:], F32),
        in_specs=[VMEM] * (len(pieces) + len(after)),
        out_specs=VMEM,
        compiler_params=params(),
        cost_estimate=cost(1, 1),
        name="gathered",
    )(*(near_core(a) for a in (*pieces, *after)))


def terms_kernel(high_ref, low_ref, *refs):
    group_refs, (keep_ref, send_ref, hold) = refs[:-3], refs[-3:]
    row = lax.axis_index("rows")
    ranks, quarter = hold.shape[0], hold.shape[1]
    width = group_refs[0].shape[1]
    for p in range(2):
        high, low = halves(jnp.concatenate([ref[p] for ref in group_refs], axis=0))
        value = dot_t(high_ref[p], high) + (dot_t(high_ref[p], low) + dot_t(low_ref[p], high))
        hold[...] = value.reshape(ranks, quarter, value.shape[1])
        for i in range(ranks // 2):
            for ref, mask in ((keep_ref, 3 * i), (send_ref, 3 * i ^ 1)):
                piece = hold[row ^ mask]
                for group in range(len(group_refs)):
                    ref[i, group, p] = piece[:, group * width : (group + 1) * width]


def terms(front, columns, ranks, after=()):
    width = columns[0].shape[1]
    quarter = front[0].shape[1] // ranks
    out = pltpu.VMEM((ranks // 2, len(columns), 2, quarter, width), F32)
    return pl.pallas_call(
        with_after(terms_kernel, 2 + len(columns), after),
        out_shape=(out, out),
        in_specs=[VMEM] * (2 + len(columns) + len(after)),
        out_specs=(VMEM,) * 2,
        scratch_shapes=[pltpu.VMEM((ranks, quarter, len(columns) * width), F32)],
        compiler_params=params(),
        cost_estimate=cost(1, 1),
        name="terms",
    )(*(near_core(a) for a in (*front, *columns, *after)))


def fold_kernel(keep_ref, got_ref, own_ref, send_ref):
    own_ref[...] = keep_ref[0] + got_ref[0]
    send_ref[...] = keep_ref[1] + got_ref[1]


def fold(keep, got, after=()):
    out = pltpu.VMEM(keep.shape[1:], F32)
    return pl.pallas_call(
        with_after(fold_kernel, 2, after),
        out_shape=(out, out),
        in_specs=[VMEM] * (2 + len(after)),
        out_specs=(VMEM,) * 2,
        compiler_params=params(),
        cost_estimate=cost(1, 1),
        name="fold",
    )(*(near_core(a) for a in (keep, got, *after)))


def target_kernel(off_ref, noise_ref, out_ref, window, hold, sems):
    ranks, quarter, rows = hold.shape
    span = window.shape[1]
    copies, shifts = [], []
    for p in range(2):
        offset = jnp.clip(off_ref[p], 0, noise_ref.shape[0] - rows)
        start = jnp.minimum((offset // 8) * 8, noise_ref.shape[0] - span)
        shifts.append(offset - start)
        copies.append(
            pltpu.make_async_copy(
                noise_ref.at[pl.ds(pl.multiple_of(start, 8), span), :], window.at[p], sems.at[p]
            )
        )
    for copy in copies:
        copy.start()
    for p in range(2):
        copies[p].wait()
        turned = window[p, pl.ds(shifts[p], rows), :].T
        hold[...] = turned.reshape(ranks, quarter, rows)
        out_ref[p] = hold[lax.axis_index("rows")]


def targets(offsets, noise, rows, ranks, after=()):
    cols_here = noise.shape[1]
    quarter = cols_here // ranks
    return pl.pallas_call(
        with_after(target_kernel, 2, after),
        out_shape=pltpu.VMEM((2, quarter, rows), F32),
        in_specs=[SMEM, ANY] + [VMEM] * len(after),
        out_specs=VMEM,
        scratch_shapes=[
            pltpu.VMEM((2, rows + 8, cols_here), F32),
            pltpu.VMEM((ranks, quarter, rows), F32),
            pltpu.SemaphoreType.DMA((2,)),
        ],
        cost_estimate=cost(1, 1),
        compiler_params=params(),
        name="targets",
    )(offsets, far_memory(noise), *(near_core(a) for a in after))


def assemble_kernel(ranks, samples, masks, inv_ref, inner_ref, cross_ref, *rest):
    shares, (high_ref, low_ref, mats) = rest[: len(masks)], rest[len(masks) :]
    row, sample, group = (lax.axis_index(a) for a in ("rows", "samples", "groups"))
    rows_here = inv_ref.shape[1]
    piece = shares[0].shape[2]
    own = pl.ds(pl.multiple_of(row * rows_here, rows_here), rows_here)
    mats[0:4, own, :] = inv_ref[...]
    mats[4:6, own, :] = inner_ref[...]
    mats[6:10, own, :] = cross_ref[...]
    for pair, ref in zip(masks, shares):
        for j, (group_mask, sample_mask) in enumerate(pair):
            part = (group ^ group_mask) * samples + (sample ^ sample_mask)
            for i, k in enumerate((3, 1, 2)):
                start = (row ^ k) * rows_here + part * piece
                mats[:, pl.ds(pl.multiple_of(start, piece), piece), :] = ref[3 * j + i]
    for m in range(10):
        high_ref[m], low_ref[m] = halves(mats[m])


def assemble(inverse, inner, cross, masks, shares, ranks, samples):
    block = inverse.shape[2]
    out = pltpu.VMEM((10, block, block), B16)
    return pl.pallas_call(
        functools.partial(assemble_kernel, ranks, samples, masks),
        out_shape=(out, out),
        in_specs=[VMEM] * (3 + len(shares)),
        out_specs=(VMEM, VMEM),
        scratch_shapes=[pltpu.VMEM((10, block, block), F32)],
        cost_estimate=cost(1, 1),
        compiler_params=params(),
        name="assemble",
    )(*(near_core(a) for a in (inverse, inner, cross, *shares)))


def solve_kernel(ranks, samples, target_ref, high_ref, low_ref, *refs):
    (kept_ref, got_ref), outs, (sums, ordered) = refs[:2], refs[2 : 2 + ranks], refs[2 + ranks :]
    row, sample = lax.axis_index("rows"), lax.axis_index("samples")
    block = high_ref.shape[1]
    rows_here = block // ranks
    for i in range(samples):
        sums[sample ^ i] = kept_ref[i] + got_ref[i]
    cols = block // samples
    rest = [[None, None], [None, None]]
    for p in range(2):
        for b in range(2):
            value = jnp.concatenate(
                [sums[s, p, :, b * cols : (b + 1) * cols] for s in range(samples)], axis=-1
            )
            rest[p][b] = target_ref[p, :, b * block : (b + 1) * block] - value

    def apply(value, m):
        return stacked(dot_t, value, high_ref[m], low_ref[m])

    def link(value, m):
        return stacked(dot_n, value, high_ref[m], low_ref[m])

    x11 = apply(rest[1][1], 3)
    x10 = apply(rest[1][0] - link(x11, 5), 2)
    x01 = apply(rest[0][1] - link(x11, 9) - link(x10, 8), 1)
    x00 = apply(rest[0][0] - link(x11, 7) - link(x10, 6) - link(x01, 4), 0)
    for j in range(ranks):
        ordered[j] = jnp.concatenate(
            [x[:, j * rows_here : (j + 1) * rows_here] for x in (x00, x01, x10, x11)], axis=-1
        )
    for k, out in enumerate(outs):
        out[...] = ordered[row ^ k]


def solve(target, mats, parts, ranks, samples):
    quarter = target.shape[1]
    block = mats[0].shape[1]
    out = pltpu.VMEM((quarter, 4 * block // ranks), F32)
    return pl.pallas_call(
        functools.partial(solve_kernel, ranks, samples),
        out_shape=(out,) * ranks,
        in_specs=[VMEM] * 5,
        out_specs=(VMEM,) * ranks,
        scratch_shapes=[
            pltpu.VMEM((samples, 2, quarter, 2 * block // samples), F32),
            pltpu.VMEM((ranks, quarter, 4 * block // ranks), F32),
        ],
        cost_estimate=cost(1, 1),
        compiler_params=params(),
        name="solve",
    )(*(near_core(a) for a in (target, *mats, *parts)))


def place_kernel(ranks, *refs):
    pieces, out_ref, hold = refs[:ranks], refs[ranks], refs[ranks + 1]
    for k, ref in enumerate(pieces):
        hold[lax.axis_index("rows") ^ k] = ref[...]
    quarter, width = hold.shape[1:]
    turned = hold[...].reshape(ranks * quarter, width).T
    rows_here = out_ref.shape[2]
    for p in range(2):
        for b in range(2):
            start = (2 * p + b) * rows_here
            out_ref[p, b] = turned[start : start + rows_here]


def place(pieces):
    ranks = len(pieces)
    quarter, width = pieces[0].shape
    return pl.pallas_call(
        functools.partial(place_kernel, ranks),
        out_shape=jax.ShapeDtypeStruct((2, 2, width // 4, ranks * quarter), F32),
        in_specs=[VMEM] * ranks,
        out_specs=VMEM,
        scratch_shapes=[pltpu.VMEM((ranks, quarter, width), F32)],
        compiler_params=params(),
        cost_estimate=cost(1, 1),
        name="place",
    )(*(near_core(a) for a in pieces))


def paired(groups, ranks, samples):
    def over_rows(pieces):
        return [pieces[0]] + [exchange(pieces[k], "rows", k, ranks) for k in range(1, ranks)]

    def local(ancestor, panels, row_map, offsets, noise, inverse, inner_link, cross_link):
        block = inverse.shape[3]
        inverse = inverse.reshape((4,) + inverse.shape[2:])
        cross = cross_link.reshape((4,) + cross_link.shape[2:])
        own = jnp.swapaxes(panels, 2, 3)
        own = own.reshape((2, 2 * own.shape[2], own.shape[3]))

        share, fetched, moved = own_share(
            inverse, inner_link, cross, (ancestor, own), groups, samples
        )
        share = share[None]
        across = exchange(share, "rows", 3, ranks)
        far = exchange(moved, "samples", 2, samples)
        near = exchange(moved, "samples", 1, samples)
        front = front_rows(row_map, fetched)
        pair = gathered([share, across], front)
        beside = exchange(pair, "rows", 1, ranks)
        target = targets(offsets, noise, 2 * block, ranks, (pair,))
        far = gathered([far], (pair,))
        far_near = exchange(far, "samples", 1, samples)
        kept, sent = terms(front, (moved, near, far, far_near), ranks, (target,))
        got = exchange(sent, "rows", 1, ranks)
        here = gathered([across, beside], (sent,))
        over_x = exchange(here, "samples", 2, samples)
        over_y = exchange(here, "groups", 1, groups)
        over_xy = lax.ppermute(
            here,
            ("groups", "samples"),
            [(i, i ^ (samples + 2)) for i in range(groups * samples)],
        )
        kept, sent = fold(kept, got, ())
        came = exchange(sent, "rows", 3, ranks)
        half = gathered([here, over_x], (kept,))
        half_near = exchange(half, "samples", 1, samples)
        rest = gathered([over_y, over_xy], (half, came))
        rest_near = exchange(rest, "samples", 1, samples)
        shares = (half, rest, half_near, rest_near)
        masks = (((0, 0), (0, 2)), ((1, 0), (1, 2)), ((0, 1), (0, 3)), ((1, 1), (1, 3)))
        mats = assemble(inverse, inner_link, cross, masks, shares, ranks, samples)

        return place(over_rows(solve(target, mats, (kept, came), ranks, samples)))

    return local


def solution(mesh):
    groups, ranks, samples = (mesh.shape[a] for a in ("groups", "rows", "samples"))
    placed = (
        P(("groups", "rows"), "samples"),
        P(None, None, "rows", "samples"),
        P(None, "rows"),
        P(),
        P("groups", "samples"),
        P(None, None, "rows", None),
        P(None, "rows", None),
        P(None, None, "rows", None),
    )

    def whole(*arrays):
        block, columns = arrays[5].shape[3], arrays[0].shape[1]
        fits = (
            groups == 2
            and samples == 4
            and ranks == 4
            and block % (ranks * groups * samples * 8) == 0
            and columns % (samples * ranks * 8) == 0
        )
        return jax.shard_map(
            paired(groups, ranks, samples) if fits else general,
            mesh=mesh,
            in_specs=placed,
            out_specs=P(None, None, "rows", ("groups", "samples")),
            check_vma=False,
        )(*arrays)

    return whole
```

```python
import functools

import jax
import jax.numpy as jnp
from jax import lax
from jax.experimental import pallas as pl
from jax.experimental.pallas import tpu as pltpu
from jax.sharding import PartitionSpec as P

F32 = jnp.float32
HIGHEST = lax.Precision.HIGHEST
B16 = jnp.bfloat16
VMEM = pl.BlockSpec(memory_space=pltpu.VMEM)
SMEM = pl.BlockSpec(memory_space=pltpu.SMEM)
ANY = pl.BlockSpec(memory_space=pl.ANY)


def product(left, right):
    return jnp.dot(left, right, precision=HIGHEST, preferred_element_type=F32)


def apply_inverse(target, partial_value, inverse_rows):
    rows_here = inverse_rows.shape[0]
    share = lax.psum_scatter(partial_value, "rows", scatter_dimension=0, tiled=True)
    first_own = lax.axis_index("rows") * rows_here
    residue = lax.dynamic_slice_in_dim(target, first_own, rows_here, 0) - share
    return product(inverse_rows, lax.all_gather(residue, "rows", axis=0, tiled=True))


def general(ancestor, panels, row_map, offsets, noise, inverse, inner_link, cross_link):
    block_rows = inverse.shape[3]
    solved = [[None, None], [None, None]]
    for p in (1, 0):
        front_rows = jnp.take(ancestor, row_map[p], axis=0)
        window = lax.dynamic_slice_in_dim(noise, offsets[p], 2 * block_rows, 0)
        for b in (1, 0):
            whole = lax.all_gather(panels[p, b], "samples", axis=1, tiled=True)
            partial_value = product(whole.T, front_rows)
            if b == 0:
                partial_value = partial_value + product(inner_link[p].T, solved[p][1])
            if p == 0:
                for earlier in (0, 1):
                    partial_value = partial_value + product(
                        cross_link[b, earlier].T, solved[1][earlier]
                    )
            target = window[b * block_rows : (b + 1) * block_rows]
            solved[p][b] = apply_inverse(target, partial_value, inverse[p, b])
    return jnp.stack([jnp.stack(solved[0]), jnp.stack(solved[1])])


def exchange(array, axis, mask, size):
    return lax.ppermute(array, axis, [(i, i ^ mask) for i in range(size)])


def with_after(kernel, count, after):
    extra = len(after)

    def body(*refs):
        return kernel(*refs[:count], *refs[count + extra :])

    return body


def near_core(array):
    return pltpu.with_memory_space_constraint(array, pltpu.VMEM)


def far_memory(array):
    return pltpu.with_memory_space_constraint(array, pltpu.HBM)


def params():
    return pltpu.CompilerParams(vmem_limit_bytes=16 * 2**20)


def cost(flops, moved):
    return pl.CostEstimate(flops=flops, bytes_accessed=moved, transcendentals=0)


def halves(value):
    high = value.astype(B16)
    return high, (value - high.astype(F32)).astype(B16)


def dot_t(left, right):
    return lax.dot_general(left, right, (((1,), (1,)), ((), ())), preferred_element_type=F32)


def dot_n(left, right):
    return lax.dot_general(left, right, (((1,), (0,)), ((), ())), preferred_element_type=F32)


def stacked(dot, left, high, low):
    rows = left.shape[0]
    left_high, left_low = halves(left)
    value = dot(jnp.concatenate([left_high, left_low], axis=0), high)
    return value[:rows] + value[rows:] + dot(left_high, low)


def share_kernel(samples, *refs):
    sources, (share_ref, *fetched), sems = refs[:5], refs[5:8], refs[8]
    inv_ref, inner_ref, cross_ref, *whole = sources
    piece = share_ref.shape[1]
    part = lax.axis_index("groups") * samples + lax.axis_index("samples")
    rows = pl.ds(pl.multiple_of(part * piece, piece), piece)
    pairs, at = [], 0
    for ref in (inv_ref, inner_ref, cross_ref):
        pairs.append((ref.at[:, rows, :], share_ref.at[at : at + ref.shape[0]]))
        at += ref.shape[0]
    pairs += list(zip(whole, fetched))
    copies = [pltpu.make_async_copy(*pair, sems.at[i]) for i, pair in enumerate(pairs)]
    for copy in copies:
        copy.start()
    for copy in copies:
        copy.wait()


def own_share(inverse, inner, cross, whole, groups, samples):
    parts = groups * samples
    rows_here, block = inverse.shape[1:]
    return pl.pallas_call(
        functools.partial(share_kernel, samples),
        out_shape=(pltpu.VMEM((10, rows_here // parts, block), F32),)
        + tuple(pltpu.VMEM(a.shape, a.dtype) for a in whole),
        in_specs=[ANY] * (3 + len(whole)),
        out_specs=(VMEM,) * (1 + len(whole)),
        scratch_shapes=[pltpu.SemaphoreType.DMA((3 + len(whole),))],
        compiler_params=params(),
        cost_estimate=cost(1265000000, 1),
        name="own_share",
    )(*(far_memory(a) for a in (inverse, inner, cross, *whole)))


def front_kernel(map_ref, ancestor_ref, high_ref, low_ref, front):
    k_rows = front.shape[1]
    step = 8
    for p in range(2):

        def body(i, carry):
            base = pl.multiple_of(i * step, step)
            rows = [ancestor_ref[pl.ds(map_ref[p, base + j], 1), :] for j in range(step)]
            front[p, pl.ds(base, step), :] = jnp.concatenate(rows, axis=0)
            return carry

        lax.fori_loop(0, k_rows // step, body, 0, unroll=8)
        high_ref[p], low_ref[p] = halves(front[p].T)


def front_rows(row_map, ancestor):
    k_rows, cols_here = row_map.shape[1], ancestor.shape[1]
    out = pltpu.VMEM((2, cols_here, k_rows), B16)
    return pl.pallas_call(
        front_kernel,
        out_shape=(out, out),
        in_specs=[SMEM, VMEM],
        out_specs=(VMEM, VMEM),
        scratch_shapes=[pltpu.VMEM((2, k_rows, cols_here), F32)],
        cost_estimate=cost(2300000000, 1),
        compiler_params=params(),
        name="front_rows",
    )(far_memory(row_map), near_core(ancestor))


def gather_kernel(count, *refs):
    pieces, out_ref = refs[:count], refs[-1]
    at = 0
    for ref in pieces:
        out_ref[at : at + ref.shape[0]] = ref[...]
        at += ref.shape[0]


def gathered(pieces, after):
    total = sum(piece.shape[0] for piece in pieces)
    return pl.pallas_call(
        functools.partial(gather_kernel, len(pieces)),
        out_shape=pltpu.VMEM((total,) + pieces[0].shape[1:], F32),
        in_specs=[VMEM] * (len(pieces) + len(after)),
        out_specs=VMEM,
        compiler_params=params(),
        cost_estimate=cost(115000000, 1),
        name="gathered",
    )(*(near_core(a) for a in (*pieces, *after)))


def terms_kernel(high_ref, low_ref, *refs):
    group_refs, (keep_ref, send_ref, hold) = refs[:-3], refs[-3:]
    row = lax.axis_index("rows")
    ranks, quarter = hold.shape[0], hold.shape[1]
    width = group_refs[0].shape[1]
    for p in range(2):
        high, low = halves(jnp.concatenate([ref[p] for ref in group_refs], axis=0))
        value = dot_t(high_ref[p], high) + (dot_t(high_ref[p], low) + dot_t(low_ref[p], high))
        hold[...] = value.reshape(ranks, quarter, value.shape[1])
        for i in range(ranks // 2):
            for ref, mask in ((keep_ref, 3 * i), (send_ref, 3 * i ^ 1)):
                piece = hold[row ^ mask]
                for group in range(len(group_refs)):
                    ref[i, group, p] = piece[:, group * width : (group + 1) * width]


def terms(front, columns, ranks, after=()):
    width = columns[0].shape[1]
    quarter = front[0].shape[1] // ranks
    out = pltpu.VMEM((ranks // 2, len(columns), 2, quarter, width), F32)
    return pl.pallas_call(
        with_after(terms_kernel, 2 + len(columns), after),
        out_shape=(out, out),
        in_specs=[VMEM] * (2 + len(columns) + len(after)),
        out_specs=(VMEM,) * 2,
        scratch_shapes=[pltpu.VMEM((ranks, quarter, len(columns) * width), F32)],
        compiler_params=params(),
        cost_estimate=cost(805000000, 1),
        name="terms",
    )(*(near_core(a) for a in (*front, *columns, *after)))


def fold_kernel(keep_1, got_1, keep_2, got_2, own_ref, send_ref):
    groups = keep_1.shape[1]
    for i, (keep_ref, got_ref) in enumerate(((keep_1, got_1), (keep_2, got_2))):
        at = slice(i * groups, (i + 1) * groups)
        own_ref[at] = keep_ref[0] + got_ref[0]
        send_ref[at] = keep_ref[1] + got_ref[1]


def fold(parts, after=()):
    shape = parts[0].shape
    out = pltpu.VMEM((2 * shape[1],) + shape[2:], F32)
    return pl.pallas_call(
        with_after(fold_kernel, 4, after),
        out_shape=(out, out),
        in_specs=[VMEM] * (4 + len(after)),
        out_specs=(VMEM,) * 2,
        compiler_params=params(),
        cost_estimate=cost(115000000, 1),
        name="fold",
    )(*(near_core(a) for a in (*parts, *after)))


def target_kernel(off_ref, noise_ref, out_ref, window, hold, sems):
    ranks, quarter, rows = hold.shape
    span = window.shape[1]
    copies, shifts = [], []
    for p in range(2):
        offset = jnp.clip(off_ref[p], 0, noise_ref.shape[0] - rows)
        start = jnp.minimum((offset // 8) * 8, noise_ref.shape[0] - span)
        shifts.append(offset - start)
        copies.append(
            pltpu.make_async_copy(
                noise_ref.at[pl.ds(pl.multiple_of(start, 8), span), :], window.at[p], sems.at[p]
            )
        )
    for copy in copies:
        copy.start()
    for p in range(2):
        copies[p].wait()
        turned = window[p, pl.ds(shifts[p], rows), :].T
        hold[...] = turned.reshape(ranks, quarter, rows)
        out_ref[p] = hold[lax.axis_index("rows")]


def targets(offsets, noise, rows, ranks, after=()):
    cols_here = noise.shape[1]
    quarter = cols_here // ranks
    return pl.pallas_call(
        with_after(target_kernel, 2, after),
        out_shape=pltpu.VMEM((2, quarter, rows), F32),
        in_specs=[SMEM, ANY] + [VMEM] * len(after),
        out_specs=VMEM,
        scratch_shapes=[
            pltpu.VMEM((2, rows + 8, cols_here), F32),
            pltpu.VMEM((ranks, quarter, rows), F32),
            pltpu.SemaphoreType.DMA((2,)),
        ],
        cost_estimate=cost(2070000000, 1),
        compiler_params=params(),
        name="targets",
    )(offsets, far_memory(noise), *(near_core(a) for a in after))


def assemble_kernel(ranks, samples, masks, inv_ref, inner_ref, cross_ref, *rest):
    shares, (high_ref, low_ref, mats) = rest[: len(masks)], rest[len(masks) :]
    row, sample, group = (lax.axis_index(a) for a in ("rows", "samples", "groups"))
    rows_here = inv_ref.shape[1]
    piece = shares[0].shape[2]
    own = pl.ds(pl.multiple_of(row * rows_here, rows_here), rows_here)
    mats[0:4, own, :] = inv_ref[...]
    mats[4:6, own, :] = inner_ref[...]
    mats[6:10, own, :] = cross_ref[...]
    for pair, ref in zip(masks, shares):
        for j, (group_mask, sample_mask) in enumerate(pair):
            part = (group ^ group_mask) * samples + (sample ^ sample_mask)
            for i, k in enumerate((3, 1, 2)):
                start = (row ^ k) * rows_here + part * piece
                mats[:, pl.ds(pl.multiple_of(start, piece), piece), :] = ref[3 * j + i]
    for m in range(10):
        high_ref[m], low_ref[m] = halves(mats[m])


def assemble(inverse, inner, cross, masks, shares, ranks, samples):
    block = inverse.shape[2]
    out = pltpu.VMEM((10, block, block), B16)
    return pl.pallas_call(
        functools.partial(assemble_kernel, ranks, samples, masks),
        out_shape=(out, out),
        in_specs=[VMEM] * (3 + len(shares)),
        out_specs=(VMEM, VMEM),
        scratch_shapes=[pltpu.VMEM((10, block, block), F32)],
        cost_estimate=cost(920000000, 1),
        compiler_params=params(),
        name="assemble",
    )(*(near_core(a) for a in (inverse, inner, cross, *shares)))


def solve_kernel(ranks, samples, target_ref, high_ref, low_ref, *refs):
    (kept_ref, got_ref), outs, (sums, ordered) = refs[:2], refs[2 : 2 + ranks], refs[2 + ranks :]
    row, sample = lax.axis_index("rows"), lax.axis_index("samples")
    block = high_ref.shape[1]
    rows_here = block // ranks
    for i in range(samples):
        sums[sample ^ i] = kept_ref[i] + got_ref[i]
    cols = block // samples
    rest = [[None, None], [None, None]]
    for p in range(2):
        for b in range(2):
            value = jnp.concatenate(
                [sums[s, p, :, b * cols : (b + 1) * cols] for s in range(samples)], axis=-1
            )
            rest[p][b] = target_ref[p, :, b * block : (b + 1) * block] - value

    def apply(value, m):
        return stacked(dot_t, value, high_ref[m], low_ref[m])

    def link(value, m):
        return stacked(dot_n, value, high_ref[m], low_ref[m])

    x11 = apply(rest[1][1], 3)
    x10 = apply(rest[1][0] - link(x11, 5), 2)
    x01 = apply(rest[0][1] - link(x11, 9) - link(x10, 8), 1)
    x00 = apply(rest[0][0] - link(x11, 7) - link(x10, 6) - link(x01, 4), 0)
    for j in range(ranks):
        ordered[j] = jnp.concatenate(
            [x[:, j * rows_here : (j + 1) * rows_here] for x in (x00, x01, x10, x11)], axis=-1
        )
    for k, out in enumerate(outs):
        out[...] = ordered[row ^ k]


def solve(target, mats, parts, ranks, samples):
    quarter = target.shape[1]
    block = mats[0].shape[1]
    out = pltpu.VMEM((quarter, 4 * block // ranks), F32)
    return pl.pallas_call(
        functools.partial(solve_kernel, ranks, samples),
        out_shape=(out,) * ranks,
        in_specs=[VMEM] * 5,
        out_specs=(VMEM,) * ranks,
        scratch_shapes=[
            pltpu.VMEM((samples, 2, quarter, 2 * block // samples), F32),
            pltpu.VMEM((ranks, quarter, 4 * block // ranks), F32),
        ],
        cost_estimate=cost(1610000000, 1),
        compiler_params=params(),
        name="solve",
    )(*(near_core(a) for a in (target, *mats, *parts)))


def place_kernel(ranks, *refs):
    pieces, out_ref, hold = refs[:ranks], refs[ranks], refs[ranks + 1]
    for k, ref in enumerate(pieces):
        hold[lax.axis_index("rows") ^ k] = ref[...]
    quarter, width = hold.shape[1:]
    turned = hold[...].reshape(ranks * quarter, width).T
    rows_here = out_ref.shape[2]
    for p in range(2):
        for b in range(2):
            start = (2 * p + b) * rows_here
            out_ref[p, b] = turned[start : start + rows_here]


def place(pieces):
    ranks = len(pieces)
    quarter, width = pieces[0].shape
    return pl.pallas_call(
        functools.partial(place_kernel, ranks),
        out_shape=jax.ShapeDtypeStruct((2, 2, width // 4, ranks * quarter), F32),
        in_specs=[VMEM] * ranks,
        out_specs=VMEM,
        scratch_shapes=[pltpu.VMEM((ranks, quarter, width), F32)],
        compiler_params=params(),
        cost_estimate=cost(920000000, 1),
        name="place",
    )(*(near_core(a) for a in pieces))


def paired(groups, ranks, samples):
    def over_rows(pieces):
        return [pieces[0]] + [exchange(pieces[k], "rows", k, ranks) for k in range(1, ranks)]

    def local(ancestor, panels, row_map, offsets, noise, inverse, inner_link, cross_link):
        block = inverse.shape[3]
        inverse = inverse.reshape((4,) + inverse.shape[2:])
        cross = cross_link.reshape((4,) + cross_link.shape[2:])
        own = jnp.swapaxes(panels, 2, 3)
        own = own.reshape((2, 2 * own.shape[2], own.shape[3]))

        share, fetched, moved = own_share(
            inverse, inner_link, cross, (ancestor, own), groups, samples
        )
        share = share[None]
        far = exchange(own, "samples", 2, samples)
        across = exchange(share, "rows", 3, ranks)
        near = exchange(moved, "samples", 1, samples)
        front = front_rows(row_map, fetched)
        pair = gathered([share, across], front)
        beside = exchange(pair, "rows", 1, ranks)
        kept_1, sent_1 = terms(front, (moved, near), ranks, ())
        got_1 = exchange(sent_1, "rows", 1, ranks)
        target = targets(offsets, noise, 2 * block, ranks, (pair,))
        far = gathered([far], (pair,))
        far_near = exchange(far, "samples", 1, samples)
        here = gathered([across, beside], (sent_1,))
        kept_2, sent_2 = terms(front, (far, far_near), ranks, (target, here))
        got_2 = exchange(sent_2, "rows", 1, ranks)
        over_x = exchange(here, "samples", 2, samples)
        over_y = exchange(here, "groups", 1, groups)
        over_xy = lax.ppermute(
            here,
            ("groups", "samples"),
            [(i, i ^ (samples + 2)) for i in range(groups * samples)],
        )
        kept, sent = fold((kept_1, got_1, kept_2, got_2), ())
        came = exchange(sent, "rows", 3, ranks)
        half = gathered([here, over_x, over_y, over_xy], (came,))
        half_near = exchange(half, "samples", 1, samples)
        shares = (half, half_near)
        masks = (((0, 0), (0, 2), (1, 0), (1, 2)), ((0, 1), (0, 3), (1, 1), (1, 3)))
        mats = assemble(inverse, inner_link, cross, masks, shares, ranks, samples)

        return place(over_rows(solve(target, mats, (kept, came), ranks, samples)))

    return local


def solution(mesh):
    groups, ranks, samples = (mesh.shape[a] for a in ("groups", "rows", "samples"))
    placed = (
        P(("groups", "rows"), "samples"),
        P(None, None, "rows", "samples"),
        P(None, "rows"),
        P(),
        P("groups", "samples"),
        P(None, None, "rows", None),
        P(None, "rows", None),
        P(None, None, "rows", None),
    )

    def whole(*arrays):
        block, columns = arrays[5].shape[3], arrays[0].shape[1]
        fits = (
            groups == 2
            and samples == 4
            and ranks == 4
            and block % (ranks * groups * samples * 8) == 0
            and columns % (samples * ranks * 8) == 0
        )
        return jax.shard_map(
            paired(groups, ranks, samples) if fits else general,
            mesh=mesh,
            in_specs=placed,
            out_specs=P(None, None, "rows", ("groups", "samples")),
            check_vma=False,
        )(*arrays)

    return whole
```

```python
import functools

import jax
import jax.numpy as jnp
from jax import lax
from jax.experimental import pallas as pl
from jax.experimental.pallas import tpu as pltpu
from jax.sharding import PartitionSpec as P

F32 = jnp.float32
HIGHEST = lax.Precision.HIGHEST
B16 = jnp.bfloat16
VMEM = pl.BlockSpec(memory_space=pltpu.VMEM)
SMEM = pl.BlockSpec(memory_space=pltpu.SMEM)
ANY = pl.BlockSpec(memory_space=pl.ANY)


def product(left, right):
    return jnp.dot(left, right, precision=HIGHEST, preferred_element_type=F32)


def apply_inverse(target, partial_value, inverse_rows):
    rows_here = inverse_rows.shape[0]
    share = lax.psum_scatter(partial_value, "rows", scatter_dimension=0, tiled=True)
    first_own = lax.axis_index("rows") * rows_here
    residue = lax.dynamic_slice_in_dim(target, first_own, rows_here, 0) - share
    return product(inverse_rows, lax.all_gather(residue, "rows", axis=0, tiled=True))


def general(ancestor, panels, row_map, offsets, noise, inverse, inner_link, cross_link):
    block_rows = inverse.shape[3]
    solved = [[None, None], [None, None]]
    for p in (1, 0):
        front_rows = jnp.take(ancestor, row_map[p], axis=0)
        window = lax.dynamic_slice_in_dim(noise, offsets[p], 2 * block_rows, 0)
        for b in (1, 0):
            whole = lax.all_gather(panels[p, b], "samples", axis=1, tiled=True)
            partial_value = product(whole.T, front_rows)
            if b == 0:
                partial_value = partial_value + product(inner_link[p].T, solved[p][1])
            if p == 0:
                for earlier in (0, 1):
                    partial_value = partial_value + product(
                        cross_link[b, earlier].T, solved[1][earlier]
                    )
            target = window[b * block_rows : (b + 1) * block_rows]
            solved[p][b] = apply_inverse(target, partial_value, inverse[p, b])
    return jnp.stack([jnp.stack(solved[0]), jnp.stack(solved[1])])


def exchange(array, axis, mask, size):
    return lax.ppermute(array, axis, [(i, i ^ mask) for i in range(size)])


def with_after(kernel, count, after):
    extra = len(after)

    def body(*refs):
        return kernel(*refs[:count], *refs[count + extra :])

    return body


def near_core(array):
    return pltpu.with_memory_space_constraint(array, pltpu.VMEM)


def far_memory(array):
    return pltpu.with_memory_space_constraint(array, pltpu.HBM)


def params():
    return pltpu.CompilerParams(vmem_limit_bytes=16 * 2**20)


def cost(flops, moved):
    return pl.CostEstimate(flops=flops, bytes_accessed=moved, transcendentals=0)


def halves(value):
    high = value.astype(B16)
    return high, (value - high.astype(F32)).astype(B16)


def dot_t(left, right):
    return lax.dot_general(left, right, (((1,), (1,)), ((), ())), preferred_element_type=F32)


def dot_n(left, right):
    return lax.dot_general(left, right, (((1,), (0,)), ((), ())), preferred_element_type=F32)


def stacked(dot, left, high, low):
    rows = left.shape[0]
    left_high, left_low = halves(left)
    value = dot(jnp.concatenate([left_high, left_low], axis=0), high)
    return value[:rows] + value[rows:] + dot(left_high, low)


def share_kernel(samples, *refs):
    sources, (share_ref, *fetched), sems = refs[:5], refs[5:8], refs[8]
    inv_ref, inner_ref, cross_ref, *whole = sources
    piece = share_ref.shape[1]
    part = lax.axis_index("groups") * samples + lax.axis_index("samples")
    rows = pl.ds(pl.multiple_of(part * piece, piece), piece)
    pairs, at = [], 0
    for ref in (inv_ref, inner_ref, cross_ref):
        pairs.append((ref.at[:, rows, :], share_ref.at[at : at + ref.shape[0]]))
        at += ref.shape[0]
    pairs += list(zip(whole, fetched))
    copies = [pltpu.make_async_copy(*pair, sems.at[i]) for i, pair in enumerate(pairs)]
    for copy in copies:
        copy.start()
    for copy in copies:
        copy.wait()


def own_share(inverse, inner, cross, whole, groups, samples):
    parts = groups * samples
    rows_here, block = inverse.shape[1:]
    return pl.pallas_call(
        functools.partial(share_kernel, samples),
        out_shape=(pltpu.VMEM((10, rows_here // parts, block), F32),)
        + tuple(pltpu.VMEM(a.shape, a.dtype) for a in whole),
        in_specs=[ANY] * (3 + len(whole)),
        out_specs=(VMEM,) * (1 + len(whole)),
        scratch_shapes=[pltpu.SemaphoreType.DMA((3 + len(whole),))],
        compiler_params=params(),
        cost_estimate=cost(1265000000, 1),
        name="own_share",
    )(*(far_memory(a) for a in (inverse, inner, cross, *whole)))


def front_kernel(map_ref, ancestor_ref, high_ref, low_ref, front):
    k_rows = front.shape[1]
    step = 8
    for p in range(2):

        def body(i, carry):
            base = pl.multiple_of(i * step, step)
            rows = [ancestor_ref[pl.ds(map_ref[p, base + j], 1), :] for j in range(step)]
            front[p, pl.ds(base, step), :] = jnp.concatenate(rows, axis=0)
            return carry

        lax.fori_loop(0, k_rows // step, body, 0, unroll=8)
        high_ref[p], low_ref[p] = halves(front[p].T)


def front_rows(row_map, ancestor):
    k_rows, cols_here = row_map.shape[1], ancestor.shape[1]
    out = pltpu.VMEM((2, cols_here, k_rows), B16)
    return pl.pallas_call(
        front_kernel,
        out_shape=(out, out),
        in_specs=[SMEM, VMEM],
        out_specs=(VMEM, VMEM),
        scratch_shapes=[pltpu.VMEM((2, k_rows, cols_here), F32)],
        cost_estimate=cost(2300000000, 1),
        compiler_params=params(),
        name="front_rows",
    )(far_memory(row_map), near_core(ancestor))


def gather_kernel(count, *refs):
    pieces, out_ref = refs[:count], refs[-1]
    at = 0
    for ref in pieces:
        out_ref[at : at + ref.shape[0]] = ref[...]
        at += ref.shape[0]


def gathered(pieces, after):
    total = sum(piece.shape[0] for piece in pieces)
    return pl.pallas_call(
        functools.partial(gather_kernel, len(pieces)),
        out_shape=pltpu.VMEM((total,) + pieces[0].shape[1:], F32),
        in_specs=[VMEM] * (len(pieces) + len(after)),
        out_specs=VMEM,
        compiler_params=params(),
        cost_estimate=cost(115000000, 1),
        name="gathered",
    )(*(near_core(a) for a in (*pieces, *after)))


def terms_kernel(high_ref, low_ref, *refs):
    group_refs, (keep_ref, send_ref, hold) = refs[:-3], refs[-3:]
    row = lax.axis_index("rows")
    ranks, quarter = hold.shape[0], hold.shape[1]
    width = group_refs[0].shape[1]
    for p in range(2):
        high, low = halves(jnp.concatenate([ref[p] for ref in group_refs], axis=0))
        value = dot_t(high_ref[p], high) + (dot_t(high_ref[p], low) + dot_t(low_ref[p], high))
        hold[...] = value.reshape(ranks, quarter, value.shape[1])
        for i in range(ranks // 2):
            for ref, mask in ((keep_ref, 3 * i), (send_ref, 3 * i ^ 1)):
                piece = hold[row ^ mask]
                for group in range(len(group_refs)):
                    ref[i, group, p] = piece[:, group * width : (group + 1) * width]


def terms(front, columns, ranks, after=()):
    width = columns[0].shape[1]
    quarter = front[0].shape[1] // ranks
    out = pltpu.VMEM((ranks // 2, len(columns), 2, quarter, width), F32)
    return pl.pallas_call(
        with_after(terms_kernel, 2 + len(columns), after),
        out_shape=(out, out),
        in_specs=[VMEM] * (2 + len(columns) + len(after)),
        out_specs=(VMEM,) * 2,
        scratch_shapes=[pltpu.VMEM((ranks, quarter, len(columns) * width), F32)],
        compiler_params=params(),
        cost_estimate=cost(805000000, 1),
        name="terms",
    )(*(near_core(a) for a in (*front, *columns, *after)))


def fold_kernel(keep_1, got_1, keep_2, got_2, own_ref, send_ref):
    groups = keep_1.shape[1]
    for i, (keep_ref, got_ref) in enumerate(((keep_1, got_1), (keep_2, got_2))):
        at = slice(i * groups, (i + 1) * groups)
        own_ref[at] = keep_ref[0] + got_ref[0]
        send_ref[at] = keep_ref[1] + got_ref[1]


def fold(parts, after=()):
    shape = parts[0].shape
    out = pltpu.VMEM((2 * shape[1],) + shape[2:], F32)
    return pl.pallas_call(
        with_after(fold_kernel, 4, after),
        out_shape=(out, out),
        in_specs=[VMEM] * (4 + len(after)),
        out_specs=(VMEM,) * 2,
        compiler_params=params(),
        cost_estimate=cost(115000000, 1),
        name="fold",
    )(*(near_core(a) for a in (*parts, *after)))


def target_kernel(off_ref, noise_ref, out_ref, window, hold, sems):
    ranks, quarter, rows = hold.shape
    span = window.shape[1]
    copies, shifts = [], []
    for p in range(2):
        offset = jnp.clip(off_ref[p], 0, noise_ref.shape[0] - rows)
        start = jnp.minimum((offset // 8) * 8, noise_ref.shape[0] - span)
        shifts.append(offset - start)
        copies.append(
            pltpu.make_async_copy(
                noise_ref.at[pl.ds(pl.multiple_of(start, 8), span), :], window.at[p], sems.at[p]
            )
        )
    for copy in copies:
        copy.start()
    for p in range(2):
        copies[p].wait()
        turned = window[p, pl.ds(shifts[p], rows), :].T
        hold[...] = turned.reshape(ranks, quarter, rows)
        out_ref[p] = hold[lax.axis_index("rows")]


def targets(offsets, noise, rows, ranks, after=()):
    cols_here = noise.shape[1]
    quarter = cols_here // ranks
    return pl.pallas_call(
        with_after(target_kernel, 2, after),
        out_shape=pltpu.VMEM((2, quarter, rows), F32),
        in_specs=[SMEM, ANY] + [VMEM] * len(after),
        out_specs=VMEM,
        scratch_shapes=[
            pltpu.VMEM((2, rows + 8, cols_here), F32),
            pltpu.VMEM((ranks, quarter, rows), F32),
            pltpu.SemaphoreType.DMA((2,)),
        ],
        cost_estimate=cost(2070000000, 1),
        compiler_params=params(),
        name="targets",
    )(offsets, far_memory(noise), *(near_core(a) for a in after))


def fill(mats, masks, shares):
    row, sample, group = (lax.axis_index(a) for a in ("rows", "samples", "groups"))
    ranks, samples = lax.axis_size("rows"), lax.axis_size("samples")
    rows_here = mats.shape[1] // ranks
    piece = shares[0].shape[2]
    for pairs, ref in zip(masks, shares):
        for j, (group_mask, sample_mask) in enumerate(pairs):
            part = (group ^ group_mask) * samples + (sample ^ sample_mask)
            for i, k in enumerate((3, 1, 2)):
                start = (row ^ k) * rows_here + part * piece
                mats[:, pl.ds(pl.multiple_of(start, piece), piece), :] = ref[3 * j + i]


def fill_own(mats, inv_ref, inner_ref, cross_ref):
    rows_here = inv_ref.shape[1]
    start = lax.axis_index("rows") * rows_here
    own = pl.ds(pl.multiple_of(start, rows_here), rows_here)
    mats[0:4, own, :] = inv_ref[...]
    mats[4:6, own, :] = inner_ref[...]
    mats[6:10, own, :] = cross_ref[...]


def solve_kernel(ranks, samples, masks, target_ref, *refs):
    sources, shares, (kept_ref, got_ref) = refs[:3], refs[3:5], refs[5:7]
    outs, (sums, ordered, mats) = refs[7 : 7 + ranks], refs[7 + ranks :]
    fill_own(mats, *sources)
    fill(mats, masks, shares)
    row, sample = lax.axis_index("rows"), lax.axis_index("samples")
    block = mats.shape[1]
    rows_here = block // ranks
    for i in range(samples):
        sums[sample ^ i] = kept_ref[i] + got_ref[i]
    cols = block // samples
    rest = [[None, None], [None, None]]
    for p in range(2):
        for b in range(2):
            value = jnp.concatenate(
                [sums[s, p, :, b * cols : (b + 1) * cols] for s in range(samples)], axis=-1
            )
            rest[p][b] = target_ref[p, :, b * block : (b + 1) * block] - value

    def apply(value, m):
        return stacked(dot_t, value, *halves(mats[m]))

    def link(value, m):
        return stacked(dot_n, value, *halves(mats[m]))

    x11 = apply(rest[1][1], 3)
    x10 = apply(rest[1][0] - link(x11, 5), 2)
    x01 = apply(rest[0][1] - link(x11, 9) - link(x10, 8), 1)
    x00 = apply(rest[0][0] - link(x11, 7) - link(x10, 6) - link(x01, 4), 0)
    for j in range(ranks):
        ordered[j] = jnp.concatenate(
            [x[:, j * rows_here : (j + 1) * rows_here] for x in (x00, x01, x10, x11)], axis=-1
        )
    for k, out in enumerate(outs):
        out[...] = ordered[row ^ k]


def solve(target, matrices, masks, shares, parts, ranks, samples):
    quarter = target.shape[1]
    block = matrices[0].shape[2]
    out = pltpu.VMEM((quarter, 4 * block // ranks), F32)
    return pl.pallas_call(
        functools.partial(solve_kernel, ranks, samples, masks),
        out_shape=(out,) * ranks,
        in_specs=[VMEM] * 8,
        out_specs=(VMEM,) * ranks,
        scratch_shapes=[
            pltpu.VMEM((samples, 2, quarter, 2 * block // samples), F32),
            pltpu.VMEM((ranks, quarter, 4 * block // ranks), F32),
            pltpu.VMEM((10, block, block), F32),
        ],
        compiler_params=params(),
        cost_estimate=cost(2000000000, 1),
        name="solve",
    )(*(near_core(a) for a in (target, *matrices, *shares, *parts)))


def place_kernel(ranks, *refs):
    pieces, out_ref, hold = refs[:ranks], refs[ranks], refs[ranks + 1]
    for k, ref in enumerate(pieces):
        hold[lax.axis_index("rows") ^ k] = ref[...]
    quarter, width = hold.shape[1:]
    turned = hold[...].reshape(ranks * quarter, width).T
    rows_here = out_ref.shape[2]
    for p in range(2):
        for b in range(2):
            start = (2 * p + b) * rows_here
            out_ref[p, b] = turned[start : start + rows_here]


def place(pieces):
    ranks = len(pieces)
    quarter, width = pieces[0].shape
    return pl.pallas_call(
        functools.partial(place_kernel, ranks),
        out_shape=jax.ShapeDtypeStruct((2, 2, width // 4, ranks * quarter), F32),
        in_specs=[VMEM] * ranks,
        out_specs=VMEM,
        scratch_shapes=[pltpu.VMEM((ranks, quarter, width), F32)],
        compiler_params=params(),
        cost_estimate=cost(920000000, 1),
        name="place",
    )(*(near_core(a) for a in pieces))


def paired(groups, ranks, samples):
    def over_rows(pieces):
        return [pieces[0]] + [exchange(pieces[k], "rows", k, ranks) for k in range(1, ranks)]

    def local(ancestor, panels, row_map, offsets, noise, inverse, inner_link, cross_link):
        block = inverse.shape[3]
        inverse = inverse.reshape((4,) + inverse.shape[2:])
        cross = cross_link.reshape((4,) + cross_link.shape[2:])
        own = jnp.swapaxes(panels, 2, 3)
        own = own.reshape((2, 2 * own.shape[2], own.shape[3]))

        share, fetched, moved = own_share(
            inverse, inner_link, cross, (ancestor, own), groups, samples
        )
        share = share[None]
        far = exchange(own, "samples", 2, samples)
        across = exchange(share, "rows", 3, ranks)
        near = exchange(moved, "samples", 1, samples)
        front = front_rows(row_map, fetched)
        pair = gathered([share, across], front)
        beside = exchange(pair, "rows", 1, ranks)
        kept_1, sent_1 = terms(front, (moved, near), ranks, ())
        got_1 = exchange(sent_1, "rows", 1, ranks)
        target = targets(offsets, noise, 2 * block, ranks, (pair,))
        far = gathered([far], (pair,))
        far_near = exchange(far, "samples", 1, samples)
        here = gathered([across, beside], (sent_1,))
        kept_2, sent_2 = terms(front, (far, far_near), ranks, (target, here))
        got_2 = exchange(sent_2, "rows", 1, ranks)
        over_x = exchange(here, "samples", 2, samples)
        over_y = exchange(here, "groups", 1, groups)
        over_xy = lax.ppermute(
            here,
            ("groups", "samples"),
            [(i, i ^ (samples + 2)) for i in range(groups * samples)],
        )
        kept, sent = fold((kept_1, got_1, kept_2, got_2), ())
        came = exchange(sent, "rows", 3, ranks)
        half = gathered([here, over_x, over_y, over_xy], (came,))
        half_near = exchange(half, "samples", 1, samples)
        shares = (half, half_near)
        masks = (((0, 0), (0, 2), (1, 0), (1, 2)), ((0, 1), (0, 3), (1, 1), (1, 3)))
        matrices = (inverse, inner_link, cross)
        pieces = solve(target, matrices, masks, shares, (kept, came), ranks, samples)
        return place(over_rows(pieces))

    return local


def solution(mesh):
    groups, ranks, samples = (mesh.shape[a] for a in ("groups", "rows", "samples"))
    placed = (
        P(("groups", "rows"), "samples"),
        P(None, None, "rows", "samples"),
        P(None, "rows"),
        P(),
        P("groups", "samples"),
        P(None, None, "rows", None),
        P(None, "rows", None),
        P(None, None, "rows", None),
    )

    def whole(*arrays):
        block, columns = arrays[5].shape[3], arrays[0].shape[1]
        fits = (
            groups == 2
            and samples == 4
            and ranks == 4
            and block % (ranks * groups * samples * 8) == 0
            and columns % (samples * ranks * 8) == 0
        )
        return jax.shard_map(
            paired(groups, ranks, samples) if fits else general,
            mesh=mesh,
            in_specs=placed,
            out_specs=P(None, None, "rows", ("groups", "samples")),
            check_vma=False,
        )(*arrays)

    return whole
```

```python
import functools

import jax
import jax.numpy as jnp
from jax import lax
from jax.experimental import pallas as pl
from jax.experimental.pallas import tpu as pltpu
from jax.sharding import PartitionSpec as P

F32 = jnp.float32
HIGHEST = lax.Precision.HIGHEST
B16 = jnp.bfloat16
VMEM = pl.BlockSpec(memory_space=pltpu.VMEM)
SMEM = pl.BlockSpec(memory_space=pltpu.SMEM)
ANY = pl.BlockSpec(memory_space=pl.ANY)


def product(left, right):
    return jnp.dot(left, right, precision=HIGHEST, preferred_element_type=F32)


def apply_inverse(target, partial_value, inverse_rows):
    rows_here = inverse_rows.shape[0]
    share = lax.psum_scatter(partial_value, "rows", scatter_dimension=0, tiled=True)
    first_own = lax.axis_index("rows") * rows_here
    residue = lax.dynamic_slice_in_dim(target, first_own, rows_here, 0) - share
    return product(inverse_rows, lax.all_gather(residue, "rows", axis=0, tiled=True))


def general(ancestor, panels, row_map, offsets, noise, inverse, inner_link, cross_link):
    block_rows = inverse.shape[3]
    solved = [[None, None], [None, None]]
    for p in (1, 0):
        front_rows = jnp.take(ancestor, row_map[p], axis=0)
        window = lax.dynamic_slice_in_dim(noise, offsets[p], 2 * block_rows, 0)
        for b in (1, 0):
            whole = lax.all_gather(panels[p, b], "samples", axis=1, tiled=True)
            partial_value = product(whole.T, front_rows)
            if b == 0:
                partial_value = partial_value + product(inner_link[p].T, solved[p][1])
            if p == 0:
                for earlier in (0, 1):
                    partial_value = partial_value + product(
                        cross_link[b, earlier].T, solved[1][earlier]
                    )
            target = window[b * block_rows : (b + 1) * block_rows]
            solved[p][b] = apply_inverse(target, partial_value, inverse[p, b])
    return jnp.stack([jnp.stack(solved[0]), jnp.stack(solved[1])])


def exchange(array, axis, mask, size):
    return lax.ppermute(array, axis, [(i, i ^ mask) for i in range(size)])


def with_after(kernel, count, after):
    extra = len(after)

    def body(*refs):
        return kernel(*refs[:count], *refs[count + extra :])

    return body


def near_core(array):
    return pltpu.with_memory_space_constraint(array, pltpu.VMEM)


def far_memory(array):
    return pltpu.with_memory_space_constraint(array, pltpu.HBM)


def params():
    return pltpu.CompilerParams(vmem_limit_bytes=16 * 2**20)


def cost(flops, moved):
    return pl.CostEstimate(flops=flops, bytes_accessed=moved, transcendentals=0)


def halves(value):
    high = value.astype(B16)
    return high, (value - high.astype(F32)).astype(B16)


def dot_t(left, right):
    return lax.dot_general(left, right, (((1,), (1,)), ((), ())), preferred_element_type=F32)


def dot_n(left, right):
    return lax.dot_general(left, right, (((1,), (0,)), ((), ())), preferred_element_type=F32)


def stacked(dot, left, high, low):
    rows = left.shape[0]
    left_high, left_low = halves(left)
    value = dot(jnp.concatenate([left_high, left_low], axis=0), high)
    return value[:rows] + value[rows:] + dot(left_high, low)


def share_kernel(samples, *refs):
    sources, (share_ref, *fetched), sems = refs[:5], refs[5:8], refs[8]
    inv_ref, inner_ref, cross_ref, *whole = sources
    piece = share_ref.shape[1]
    part = lax.axis_index("groups") * samples + lax.axis_index("samples")
    rows = pl.ds(pl.multiple_of(part * piece, piece), piece)
    pairs, at = [], 0
    for ref in (inv_ref, inner_ref, cross_ref):
        pairs.append((ref.at[:, rows, :], share_ref.at[at : at + ref.shape[0]]))
        at += ref.shape[0]
    pairs += list(zip(whole, fetched))
    copies = [pltpu.make_async_copy(*pair, sems.at[i]) for i, pair in enumerate(pairs)]
    for copy in copies:
        copy.start()
    for copy in copies:
        copy.wait()


def own_share(inverse, inner, cross, whole, groups, samples):
    parts = groups * samples
    rows_here, block = inverse.shape[1:]
    return pl.pallas_call(
        functools.partial(share_kernel, samples),
        out_shape=(pltpu.VMEM((10, rows_here // parts, block), F32),)
        + tuple(pltpu.VMEM(a.shape, a.dtype) for a in whole),
        in_specs=[ANY] * (3 + len(whole)),
        out_specs=(VMEM,) * (1 + len(whole)),
        scratch_shapes=[pltpu.SemaphoreType.DMA((3 + len(whole),))],
        compiler_params=params(),
        cost_estimate=cost(1265000000, 1),
        name="own_share",
    )(*(far_memory(a) for a in (inverse, inner, cross, *whole)))


def front_kernel(map_ref, ancestor_ref, high_ref, low_ref, front):
    k_rows = front.shape[1]
    step = 8
    for p in range(2):

        def body(i, carry):
            base = pl.multiple_of(i * step, step)
            rows = [ancestor_ref[pl.ds(map_ref[p, base + j], 1), :] for j in range(step)]
            front[p, pl.ds(base, step), :] = jnp.concatenate(rows, axis=0)
            return carry

        lax.fori_loop(0, k_rows // step, body, 0, unroll=8)
        high_ref[p], low_ref[p] = halves(front[p].T)


def front_rows(row_map, ancestor):
    k_rows, cols_here = row_map.shape[1], ancestor.shape[1]
    out = pltpu.VMEM((2, cols_here, k_rows), B16)
    return pl.pallas_call(
        front_kernel,
        out_shape=(out, out),
        in_specs=[SMEM, VMEM],
        out_specs=(VMEM, VMEM),
        scratch_shapes=[pltpu.VMEM((2, k_rows, cols_here), F32)],
        cost_estimate=cost(2300000000, 1),
        compiler_params=params(),
        name="front_rows",
    )(far_memory(row_map), near_core(ancestor))


def gather_kernel(count, *refs):
    pieces, out_ref = refs[:count], refs[-1]
    at = 0
    for ref in pieces:
        out_ref[at : at + ref.shape[0]] = ref[...]
        at += ref.shape[0]


def gathered(pieces, after):
    total = sum(piece.shape[0] for piece in pieces)
    return pl.pallas_call(
        functools.partial(gather_kernel, len(pieces)),
        out_shape=pltpu.VMEM((total,) + pieces[0].shape[1:], F32),
        in_specs=[VMEM] * (len(pieces) + len(after)),
        out_specs=VMEM,
        compiler_params=params(),
        cost_estimate=cost(115000000, 1),
        name="gathered",
    )(*(near_core(a) for a in (*pieces, *after)))


def terms_kernel(high_ref, low_ref, *refs):
    group_refs, (keep_ref, send_ref, hold) = refs[:-3], refs[-3:]
    row = lax.axis_index("rows")
    ranks, quarter = hold.shape[0], hold.shape[1]
    width = group_refs[0].shape[1]
    for p in range(2):
        high, low = halves(jnp.concatenate([ref[p] for ref in group_refs], axis=0))
        value = dot_t(high_ref[p], high) + (dot_t(high_ref[p], low) + dot_t(low_ref[p], high))
        hold[...] = value.reshape(ranks, quarter, value.shape[1])
        for i in range(ranks // 2):
            for ref, mask in ((keep_ref, 3 * i), (send_ref, 3 * i ^ 1)):
                piece = hold[row ^ mask]
                for group in range(len(group_refs)):
                    ref[i, group, p] = piece[:, group * width : (group + 1) * width]


def terms(front, columns, ranks, after=()):
    width = columns[0].shape[1]
    quarter = front[0].shape[1] // ranks
    out = pltpu.VMEM((ranks // 2, len(columns), 2, quarter, width), F32)
    return pl.pallas_call(
        with_after(terms_kernel, 2 + len(columns), after),
        out_shape=(out, out),
        in_specs=[VMEM] * (2 + len(columns) + len(after)),
        out_specs=(VMEM,) * 2,
        scratch_shapes=[pltpu.VMEM((ranks, quarter, len(columns) * width), F32)],
        compiler_params=params(),
        cost_estimate=cost(805000000, 1),
        name="terms",
    )(*(near_core(a) for a in (*front, *columns, *after)))


def fold_kernel(keep_1, got_1, keep_2, got_2, own_ref, send_ref):
    groups = keep_1.shape[1]
    for i, (keep_ref, got_ref) in enumerate(((keep_1, got_1), (keep_2, got_2))):
        at = slice(i * groups, (i + 1) * groups)
        own_ref[at] = keep_ref[0] + got_ref[0]
        send_ref[at] = keep_ref[1] + got_ref[1]


def fold(parts, after=()):
    shape = parts[0].shape
    out = pltpu.VMEM((2 * shape[1],) + shape[2:], F32)
    return pl.pallas_call(
        with_after(fold_kernel, 4, after),
        out_shape=(out, out),
        in_specs=[VMEM] * (4 + len(after)),
        out_specs=(VMEM,) * 2,
        compiler_params=params(),
        cost_estimate=cost(115000000, 1),
        name="fold",
    )(*(near_core(a) for a in (*parts, *after)))


def target_kernel(off_ref, noise_ref, out_ref, window, hold, sems):
    ranks, quarter, rows = hold.shape
    span = window.shape[1]
    copies, shifts = [], []
    for p in range(2):
        offset = jnp.clip(off_ref[p], 0, noise_ref.shape[0] - rows)
        start = jnp.minimum((offset // 8) * 8, noise_ref.shape[0] - span)
        shifts.append(offset - start)
        copies.append(
            pltpu.make_async_copy(
                noise_ref.at[pl.ds(pl.multiple_of(start, 8), span), :], window.at[p], sems.at[p]
            )
        )
    for copy in copies:
        copy.start()
    for p in range(2):
        copies[p].wait()
        turned = window[p, pl.ds(shifts[p], rows), :].T
        hold[...] = turned.reshape(ranks, quarter, rows)
        out_ref[p] = hold[lax.axis_index("rows")]


def targets(offsets, noise, rows, ranks, after=()):
    cols_here = noise.shape[1]
    quarter = cols_here // ranks
    return pl.pallas_call(
        with_after(target_kernel, 2, after),
        out_shape=pltpu.VMEM((2, quarter, rows), F32),
        in_specs=[SMEM, ANY] + [VMEM] * len(after),
        out_specs=VMEM,
        scratch_shapes=[
            pltpu.VMEM((2, rows + 8, cols_here), F32),
            pltpu.VMEM((ranks, quarter, rows), F32),
            pltpu.SemaphoreType.DMA((2,)),
        ],
        cost_estimate=cost(2070000000, 1),
        compiler_params=params(),
        name="targets",
    )(offsets, far_memory(noise), *(near_core(a) for a in after))


def fill(mats, masks, shares):
    row, sample, group = (lax.axis_index(a) for a in ("rows", "samples", "groups"))
    ranks, samples = lax.axis_size("rows"), lax.axis_size("samples")
    rows_here = mats.shape[1] // ranks
    piece = shares[0].shape[2]
    for pairs, ref in zip(masks, shares):
        for j, (group_mask, sample_mask) in enumerate(pairs):
            part = (group ^ group_mask) * samples + (sample ^ sample_mask)
            for i, k in enumerate((3, 1, 2)):
                start = (row ^ k) * rows_here + part * piece
                mats[:, pl.ds(pl.multiple_of(start, piece), piece), :] = ref[3 * j + i]


def fill_own(mats, inv_ref, inner_ref, cross_ref):
    rows_here = inv_ref.shape[1]
    start = lax.axis_index("rows") * rows_here
    own = pl.ds(pl.multiple_of(start, rows_here), rows_here)
    mats[0:4, own, :] = inv_ref[...]
    mats[4:6, own, :] = inner_ref[...]
    mats[6:10, own, :] = cross_ref[...]


def assemble_kernel(masks, inv_ref, inner_ref, cross_ref, share_ref, mats):
    fill_own(mats, inv_ref, inner_ref, cross_ref)
    fill(mats, masks, (share_ref,))


def assemble(inverse, inner, cross, masks, share):
    block = inverse.shape[2]
    return pl.pallas_call(
        functools.partial(assemble_kernel, masks),
        out_shape=pltpu.VMEM((10, block, block), F32),
        in_specs=[VMEM] * 4,
        out_specs=VMEM,
        compiler_params=params(),
        cost_estimate=cost(575000000, 1),
        name="assemble",
    )(*(near_core(a) for a in (inverse, inner, cross, share)))


def solve_kernel(ranks, samples, masks, target_ref, mats, share_ref, kept_ref, got_ref, *refs):
    outs, (sums, ordered) = refs[:ranks], refs[ranks + 1 :]
    fill(mats, masks, (share_ref,))
    row, sample = lax.axis_index("rows"), lax.axis_index("samples")
    block = mats.shape[1]
    rows_here = block // ranks
    for i in range(samples):
        sums[sample ^ i] = kept_ref[i] + got_ref[i]
    cols = block // samples
    rest = [[None, None], [None, None]]
    for p in range(2):
        for b in range(2):
            value = jnp.concatenate(
                [sums[s, p, :, b * cols : (b + 1) * cols] for s in range(samples)], axis=-1
            )
            rest[p][b] = target_ref[p, :, b * block : (b + 1) * block] - value

    def apply(value, m):
        return stacked(dot_t, value, *halves(mats[m]))

    def link(value, m):
        return stacked(dot_n, value, *halves(mats[m]))

    x11 = apply(rest[1][1], 3)
    x10 = apply(rest[1][0] - link(x11, 5), 2)
    x01 = apply(rest[0][1] - link(x11, 9) - link(x10, 8), 1)
    x00 = apply(rest[0][0] - link(x11, 7) - link(x10, 6) - link(x01, 4), 0)
    for j in range(ranks):
        ordered[j] = jnp.concatenate(
            [x[:, j * rows_here : (j + 1) * rows_here] for x in (x00, x01, x10, x11)], axis=-1
        )
    for k, out in enumerate(outs):
        out[...] = ordered[row ^ k]


def solve(target, mats, masks, share, parts, ranks, samples):
    quarter = target.shape[1]
    block = mats.shape[1]
    out = pltpu.VMEM((quarter, 4 * block // ranks), F32)
    return pl.pallas_call(
        functools.partial(solve_kernel, ranks, samples, masks),
        out_shape=(out,) * ranks + (pltpu.VMEM(mats.shape, F32),),
        in_specs=[VMEM] * 5,
        out_specs=(VMEM,) * (ranks + 1),
        scratch_shapes=[
            pltpu.VMEM((samples, 2, quarter, 2 * block // samples), F32),
            pltpu.VMEM((ranks, quarter, 4 * block // ranks), F32),
        ],
        input_output_aliases={1: ranks},
        compiler_params=params(),
        cost_estimate=cost(1700000000, 1),
        name="solve",
    )(*(near_core(a) for a in (target, mats, share, *parts)))[:ranks]


def place_kernel(ranks, *refs):
    pieces, out_ref, hold = refs[:ranks], refs[ranks], refs[ranks + 1]
    for k, ref in enumerate(pieces):
        hold[lax.axis_index("rows") ^ k] = ref[...]
    quarter, width = hold.shape[1:]
    turned = hold[...].reshape(ranks * quarter, width).T
    rows_here = out_ref.shape[2]
    for p in range(2):
        for b in range(2):
            start = (2 * p + b) * rows_here
            out_ref[p, b] = turned[start : start + rows_here]


def place(pieces):
    ranks = len(pieces)
    quarter, width = pieces[0].shape
    return pl.pallas_call(
        functools.partial(place_kernel, ranks),
        out_shape=jax.ShapeDtypeStruct((2, 2, width // 4, ranks * quarter), F32),
        in_specs=[VMEM] * ranks,
        out_specs=VMEM,
        scratch_shapes=[pltpu.VMEM((ranks, quarter, width), F32)],
        compiler_params=params(),
        cost_estimate=cost(920000000, 1),
        name="place",
    )(*(near_core(a) for a in pieces))


def paired(groups, ranks, samples):
    def over_rows(pieces):
        return [pieces[0]] + [exchange(pieces[k], "rows", k, ranks) for k in range(1, ranks)]

    def local(ancestor, panels, row_map, offsets, noise, inverse, inner_link, cross_link):
        block = inverse.shape[3]
        inverse = inverse.reshape((4,) + inverse.shape[2:])
        cross = cross_link.reshape((4,) + cross_link.shape[2:])
        own = jnp.swapaxes(panels, 2, 3)
        own = own.reshape((2, 2 * own.shape[2], own.shape[3]))

        share, fetched, moved = own_share(
            inverse, inner_link, cross, (ancestor, own), groups, samples
        )
        share = share[None]
        far = exchange(own, "samples", 2, samples)
        across = exchange(share, "rows", 3, ranks)
        near = exchange(moved, "samples", 1, samples)
        front = front_rows(row_map, fetched)
        pair = gathered([share, across], front)
        beside = exchange(pair, "rows", 1, ranks)
        kept_1, sent_1 = terms(front, (moved, near), ranks, ())
        got_1 = exchange(sent_1, "rows", 1, ranks)
        target = targets(offsets, noise, 2 * block, ranks, (pair,))
        far = gathered([far], (pair,))
        far_near = exchange(far, "samples", 1, samples)
        here = gathered([across, beside], (sent_1,))
        kept_2, sent_2 = terms(front, (far, far_near), ranks, (target, here))
        got_2 = exchange(sent_2, "rows", 1, ranks)
        over_x = exchange(here, "samples", 2, samples)
        over_y = exchange(here, "groups", 1, groups)
        over_xy = lax.ppermute(
            here,
            ("groups", "samples"),
            [(i, i ^ (samples + 2)) for i in range(groups * samples)],
        )
        kept, sent = fold((kept_1, got_1, kept_2, got_2), ())
        came = exchange(sent, "rows", 3, ranks)
        half = gathered([here, over_x, over_y, over_xy], (came,))
        half_near = exchange(half, "samples", 1, samples)
        masks = (((0, 0), (0, 2), (1, 0), (1, 2)), ((0, 1), (0, 3), (1, 1), (1, 3)))
        mats = assemble(inverse, inner_link, cross, masks[:1], half)
        pieces = solve(target, mats, masks[1:], half_near, (kept, came), ranks, samples)
        return place(over_rows(pieces))

    return local


def solution(mesh):
    groups, ranks, samples = (mesh.shape[a] for a in ("groups", "rows", "samples"))
    placed = (
        P(("groups", "rows"), "samples"),
        P(None, None, "rows", "samples"),
        P(None, "rows"),
        P(),
        P("groups", "samples"),
        P(None, None, "rows", None),
        P(None, "rows", None),
        P(None, None, "rows", None),
    )

    def whole(*arrays):
        block, columns = arrays[5].shape[3], arrays[0].shape[1]
        fits = (
            groups == 2
            and samples == 4
            and ranks == 4
            and block % (ranks * groups * samples * 8) == 0
            and columns % (samples * ranks * 8) == 0
        )
        return jax.shard_map(
            paired(groups, ranks, samples) if fits else general,
            mesh=mesh,
            in_specs=placed,
            out_specs=P(None, None, "rows", ("groups", "samples")),
            check_vma=False,
        )(*arrays)

    return whole
```
